32 devices in a mesh: gx: 4 (over y, core), gy: 8 (over z, x).
Axes of the slice: x: 2, y: 2, z: 4, core: 2. Of those that a mesh axis runs over, the one named last changes fastest.
Arguments:
- tracer_adjoint: float32 [2, 50, 320, 512], P(None, None, 'gy', 'gx'), may hold values from -6 to 6
- surface_adjoint: float32 [320, 512], P('gy', 'gx'), may hold values from -6 to 6
- flow_east: float32 [50, 320, 512], P(None, 'gy', 'gx'), may hold values from -0.4 to 0.4, as said below
- flow_north: float32 [50, 320, 512], P(None, 'gy', 'gx'), may hold values from -0.4 to 0.4, as said below
- vertical_mix: float32 [49, 320, 512], P(None, 'gy', 'gx'), may hold values from 0.1 to 10
- land_mask: int32 [50, 320, 512], P(None, 'gy', 'gx'), may hold values from 0 to 1, as said below
- conduct_east: float32 [320, 512], P('gy', 'gx'), may hold values from 0 to 4, as said below
- conduct_north: float32 [320, 512], P('gy', 'gx'), may hold values from 0 to 4, as said below
- surface_diagonal: float32 [320, 512], P('gy', 'gx'), may hold values from 0.02 to 0.2
- pressure_load: float32 [2, 50], replicated, may hold values from -0.5 to 0.5
- surface_forcing: float32 [2, 50], replicated, may hold values from -0.1 to 0.1
- control_map: int32 [1664], replicated, may hold values from 0 to 319
- control_weight: float32 [1664], replicated, may hold values from 0.5 to 1.5
Outputs:
- tracer_grad: float32 [2, 50, 320, 512], P(None, None, 'gy', 'gx')
- surface_grad: float32 [320, 512], P('gy', 'gx')
- control_grad: float32 [2, 50, 320], P(None, None, ('gx', 'gy'))
The draws below stay inside these ranges and needn't reach their ends.
Inputs may be any that keep to these rules, and one draw needn't show every extreme that they name: `land_mask`: 1 marks an ocean cell and 0 land; where a cell is ocean, the cell above it is ocean too. `flow_east`: zero on every face that touches land or lies on the grid's eastern edge. `flow_north`: zero on every face that touches land or lies on the grid's northern edge. `conduct_east`: zero on faces that touch land at the surface or lie on the eastern edge, positive elsewhere. `conduct_north`: zero on faces that touch land at the surface or lie on the northern edge, positive elsewhere.
All inputs are finite; a program needn't handle non-finite values.
Results may differ from the reference program's by a relative error of at most 0.0003.
Values sent between devices are 32-bit elements; how exact they have to be, the bound alone decides.
A program may use at most 128 MiB of HBM per device.

```python
import math
import jax
import jax.numpy as jnp

K = 50
CX = 128
CY = 40
ITERS = 3
CTRL_DEV = 10
NX = 512
NY = 320
POINTS = 1664
CONTROLS = 320


def ocean_bottom(key):
    coarse = jax.random.randint(jax.random.fold_in(key, 101), (NY // 8, NX // 8), -(K // 8), K + K // 4 + 1)
    blocks = jnp.repeat(jnp.repeat(coarse, 8, axis=0), 8, axis=1)
    jitter = jax.random.randint(jax.random.fold_in(key, 102), (NY, NX), -(K // 10) - 1, K // 10 + 2)
    return jnp.clip(blocks + jitter, 0, K)


def water_levels(key):
    bottom = ocean_bottom(key)
    levels = jnp.arange(K, dtype=jnp.int32)[:, None, None]
    return levels < bottom[None]


def draw_land_mask(key, part):
    wet_level = water_levels(key)
    return wet_level.astype(jnp.int32)


def draw_flow_east(key, part):
    wet_level = water_levels(key).astype(jnp.float32)
    key = jax.random.fold_in(key, 2)
    east_wet = jnp.pad(wet_level[:, :, 1:], ((0, 0), (0, 0), (0, 1)))
    velocity = jax.random.uniform(key, (K, NY, NX), jnp.float32, -0.3, 0.3)
    return velocity * wet_level * east_wet


def draw_flow_north(key, part):
    wet_level = water_levels(key).astype(jnp.float32)
    key = jax.random.fold_in(key, 3)
    north_wet = jnp.pad(wet_level[:, 1:, :], ((0, 0), (0, 1), (0, 0)))
    velocity = jax.random.uniform(key, (K, NY, NX), jnp.float32, -0.3, 0.3)
    return velocity * wet_level * north_wet


def draw_conduct_east(key, part):
    surface_wet = (ocean_bottom(key) > 0).astype(jnp.float32)
    key = jax.random.fold_in(key, 4)
    east_wet = jnp.pad(surface_wet[:, 1:], ((0, 0), (0, 1)))
    spread = jnp.log(2.0)
    value = jnp.exp(jax.random.uniform(key, (NY, NX), jnp.float32, -spread, spread))
    return value * surface_wet * east_wet


def draw_conduct_north(key, part):
    surface_wet = (ocean_bottom(key) > 0).astype(jnp.float32)
    key = jax.random.fold_in(key, 5)
    north_wet = jnp.pad(surface_wet[1:, :], ((0, 1), (0, 0)))
    spread = jnp.log(2.0)
    value = jnp.exp(jax.random.uniform(key, (NY, NX), jnp.float32, -spread, spread))
    return value * surface_wet * north_wet


def draw_control_map(key, part):
    key = jax.random.fold_in(key, 6)
    tiles_lon = NX // CX
    tiles_lat = NY // CY
    device_count = tiles_lon * tiles_lat
    points = jnp.arange(POINTS, dtype=jnp.int32)
    first_seg = points < NX
    second_seg = points < 2 * NX
    third_seg = points < 2 * NX + NY
    column_idx = jnp.where(first_seg, points // CX, jnp.where(second_seg, (points - NX) // CX, jnp.where(third_seg, 0, tiles_lon - 1)))
    row_idx = jnp.where(first_seg, 0, jnp.where(second_seg, tiles_lat - 1, jnp.where(third_seg, (points - 2 * NX) // CY, (points - 2 * NX - NY) // CY)))
    holder = column_idx * tiles_lat + row_idx
    random_owner = jax.random.randint(jax.random.fold_in(key, 1), (POINTS,), 0, device_count)
    phase = points % 4
    owner = jnp.where(phase == 0, holder + device_count // 2, jnp.where(phase == 1, holder + 1, jnp.where(phase == 2, holder + device_count - 1, random_owner)))
    owner = owner % device_count
    slot = jax.random.randint(jax.random.fold_in(key, 2), (POINTS,), 0, CTRL_DEV)
    chosen = owner * CTRL_DEV + slot
    chosen = jnp.where(points == 0, 0, chosen)
    chosen = jnp.where(points == POINTS - 1, CONTROLS - 1, chosen)
    return chosen.astype(jnp.int32)


def block_levels(stream_key, dims, cuts, smallest, largest):
    def one(dim, blocks):
        steps = jax.random.uniform(jax.random.fold_in(jax.random.fold_in(stream_key, 6), dim), (blocks,), jnp.float32, smallest / len(cuts), largest / len(cuts))
        return jnp.repeat(jnp.exp(steps), dims[dim] // blocks).reshape((-1,) + (1,) * (len(dims) - dim - 1))

    level = one(*cuts[0])
    for cut in cuts[1:]:
        level = level * one(*cut)
    return level


def gaussian(stream_key, shape, scale, limit, pieces=(), kind=jnp.bfloat16):
    gain = block_levels(stream_key, shape, pieces, -0.22, 0.18) if pieces else 1.0
    values = jax.random.normal(stream_key, shape, jnp.float32) * scale * gain
    return jnp.minimum(jnp.maximum(values, -limit), limit).astype(kind)


def setup_inputs(seed: int = 0) -> dict:
    keys = jax.random.split(jax.random.key(seed), 14)
    tracer_adjoint = gaussian(keys[0], (2, K, NY, NX), 1.0, 6.0, ((2, 8), (3, 4)), jnp.float32)
    surface_adjoint = gaussian(keys[1], (NY, NX), 1.0, 6.0, ((0, 8), (1, 4)), jnp.float32)
    flow_east = draw_flow_east(jax.random.fold_in(keys[13], 71), 0)
    flow_north = draw_flow_north(jax.random.fold_in(keys[13], 71), 0)
    vertical_mix = jnp.clip(jnp.exp(math.log(10.0) - 4.6051702 * jax.random.uniform(keys[4], (K - 1, NY, NX), jnp.float32) ** block_levels(keys[4], (K - 1, NY, NX), ((1, 8), (2, 4)), -0.2, 0.2)), 0.1, 10.0)
    land_mask = draw_land_mask(jax.random.fold_in(keys[13], 71), 0)
    conduct_east = draw_conduct_east(jax.random.fold_in(keys[13], 71), 0)
    conduct_north = draw_conduct_north(jax.random.fold_in(keys[13], 71), 0)
    surface_diagonal = jnp.clip(jnp.exp(math.log(0.2) - 2.3025851 * jax.random.uniform(keys[8], (NY, NX), jnp.float32) ** block_levels(keys[8], (NY, NX), ((0, 8), (1, 4)), -0.2, 0.2)), 0.02, 0.2)
    pressure_load = jnp.clip(jax.random.uniform(keys[9], (2, K), jnp.float32, -0.5, 0.5), -0.5, 0.5)
    surface_forcing = jnp.clip(jax.random.uniform(keys[10], (2, K), jnp.float32, -0.1, 0.1), -0.1, 0.1)
    control_map = draw_control_map(jax.random.fold_in(keys[13], 71), 0)
    control_weight = jnp.clip(jax.random.uniform(keys[12], (POINTS,), jnp.float32, 0.5, 1.5), 0.5, 1.5)
    return {"tracer_adjoint": tracer_adjoint, "surface_adjoint": surface_adjoint, "flow_east": flow_east, "flow_north": flow_north, "vertical_mix": vertical_mix, "land_mask": land_mask, "conduct_east": conduct_east, "conduct_north": conduct_north, "surface_diagonal": surface_diagonal, "pressure_load": pressure_load, "surface_forcing": surface_forcing, "control_map": control_map, "control_weight": control_weight}


def column_solve(right_side, kappa_vert):
    levels = right_side.shape[-3]
    ratios = []
    reduced = []
    for level in range(levels):
        diag_term = 1.0
        if level > 0:
            diag_term = diag_term + kappa_vert[level - 1]
        if level < levels - 1:
            diag_term = diag_term + kappa_vert[level]
        if level == 0:
            pivot_val = diag_term
            carried = right_side[..., 0, :, :]
        else:
            pivot_val = diag_term - kappa_vert[level - 1] * ratios[level - 1]
            carried = right_side[..., level, :, :] + kappa_vert[level - 1] * reduced[level - 1]
        reduced.append(carried / pivot_val)
        if level < levels - 1:
            ratios.append(kappa_vert[level] / pivot_val)
    solution = [reduced[levels - 1]]
    for level in range(levels - 2, -1, -1):
        solution.insert(0, reduced[level] + ratios[level] * solution[0])
    return jnp.stack(solution, axis=-3)


def surface_apply(surface, conduct_east, conduct_north, surface_diagonal):
    east_side = jnp.pad(surface[:, 1:], ((0, 0), (0, 1)))
    west_side = jnp.pad(surface[:, :-1], ((0, 0), (1, 0)))
    north_side = jnp.pad(surface[1:, :], ((0, 1), (0, 0)))
    south_side = jnp.pad(surface[:-1, :], ((1, 0), (0, 0)))
    conduct_west = jnp.pad(conduct_east[:, :-1], ((0, 0), (1, 0)))
    conduct_south = jnp.pad(conduct_north[:-1, :], ((1, 0), (0, 0)))
    return (surface_diagonal * surface + conduct_east * (surface - east_side)
            + conduct_west * (surface - west_side) + conduct_north * (surface - north_side)
            + conduct_south * (surface - south_side))


def reference(tracer_adjoint, surface_adjoint, flow_east, flow_north, vertical_mix, land_mask,
              conduct_east, conduct_north, surface_diagonal, pressure_load, surface_forcing,
              control_map, control_weight):
    wet_cells = land_mask.astype(jnp.float32)
    forcing_sum = surface_adjoint + jnp.sum(surface_forcing[:, :, None, None] * wet_cells[None] * tracer_adjoint, axis=(0, 1))
    iterate = jnp.zeros_like(forcing_sum)
    remain = forcing_sum
    search = remain
    norm_now = jnp.sum(remain * remain)
    for iteration in range(ITERS):
        image = surface_apply(search, conduct_east, conduct_north, surface_diagonal)
        step_len = norm_now / jnp.sum(search * image)
        iterate = iterate + step_len * search
        remain = remain - step_len * image
        if iteration + 1 < ITERS:
            norm_next = jnp.sum(remain * remain)
            search = remain + (norm_next / norm_now) * search
            norm_now = norm_next
    solved = iterate
    kappa_vert = vertical_mix * wet_cells[1:]
    lifted = tracer_adjoint + wet_cells[None] * pressure_load[:, :, None, None] * solved[None, None]
    lam_field = wet_cells[None] * column_solve(lifted, kappa_vert)
    east_side = jnp.pad(lam_field[..., 1:], ((0, 0), (0, 0), (0, 0), (0, 1)))
    west_side = jnp.pad(lam_field[..., :-1], ((0, 0), (0, 0), (0, 0), (1, 0)))
    north_side = jnp.pad(lam_field[..., 1:, :], ((0, 0), (0, 0), (0, 1), (0, 0)))
    south_side = jnp.pad(lam_field[..., :-1, :], ((0, 0), (0, 0), (1, 0), (0, 0)))
    flow_west = jnp.pad(flow_east[..., :-1], ((0, 0), (0, 0), (1, 0)))
    flow_south = jnp.pad(flow_north[:, :-1, :], ((0, 0), (1, 0), (0, 0)))
    tracer_grad = (lam_field + 0.5 * flow_east * (east_side - lam_field)
                   + 0.5 * flow_west * (lam_field - west_side)
                   + 0.5 * flow_north * (north_side - lam_field)
                   + 0.5 * flow_south * (lam_field - south_side))
    edge_vals = jnp.concatenate([tracer_grad[:, :, 0, :], tracer_grad[:, :, -1, :],
                                 tracer_grad[:, :, :, 0], tracer_grad[:, :, :, -1]], axis=2)
    weighted = (edge_vals * control_weight).reshape(2 * K, POINTS)
    totals = jax.ops.segment_sum(weighted.T, control_map, num_segments=CONTROLS)
    control_grad = totals.T.reshape(2, K, CONTROLS)
    return tracer_grad, solved, control_grad
```

```python
import functools
import jax
import jax.numpy as jnp
from jax import lax
from jax.experimental import pallas as pl
from jax.experimental.pallas import tpu as pltpu
from jax.sharding import PartitionSpec as P

ITERS = 3
CTRL_DEV = 10
SLOT = 16
LANES = 128
MESH = pl.DeviceIdType.MESH
DIRS = ((1, 0), (-1, 0), (0, 1), (0, -1), (1, 1), (-1, 1), (1, -1), (-1, -1))
OPPOSITE = (1, 0, 3, 2, 7, 6, 5, 4)
F32 = jnp.float32
HIGHEST = lax.Precision.HIGHEST


def column_roll(value, shift):
    return pltpu.roll(value, shift, 1)


def surface_apply(e, ce, cn, dg):
    rows, cols = e.shape
    flux_e = ce * (e - pltpu.roll(e, cols - 1, 1))
    flux_n = cn * (e - pltpu.roll(e, rows - 1, 0))
    return dg * e + (flux_e - pltpu.roll(flux_e, 1, 1)) + (flux_n - pltpu.roll(flux_n, 1, 0))


def poly_add(p, q, factor):
    size = max(len(p), len(q))
    out = []
    for i in range(size):
        term = factor * q[i] if i < len(q) else None
        if i < len(p):
            term = p[i] if term is None else p[i] + term
        out.append(term)
    return out


def gradient_weights(mu):
    def inner(p, q, shift):
        total = None
        for i, pi in enumerate(p):
            for j, qj in enumerate(q):
                term = pi * qj * mu[i + j + shift]
                total = term if total is None else total + term
        return total

    one = jnp.ones_like(mu[0])
    zero = jnp.zeros_like(mu[0])
    floor = 2e-7 * mu[0]
    res, search, x = [one], [one], [zero]
    rr = mu[0]
    for it in range(ITERS):
        den = inner(search, search, 1)
        good = (den > 0) & (rr > floor)
        step = jnp.where(good, rr / jnp.where(good, den, one), zero)
        x = poly_add(x, search, step)
        if it + 1 < ITERS:
            res = poly_add(res, [zero] + search, -step)
            rr_new = jnp.maximum(inner(res, res, 0), zero)
            ratio = jnp.where(good, rr_new / jnp.where(good, rr, one), zero)
            search = poly_add(res, search, ratio)
            rr = rr_new
    return x


def step_kernel(
    tiles_lon, tiles_lat, levels,
    tracer, surface, flow_e, flow_n, mix, mask, cond_e, cond_n, diag, load, forcing, cmap, cwt,
    grad_out, surf_out, ctrl_out,
    red, ratio, quad, q_e, q_w, q_n, q_s, q_c,
    send_e, send_w, send_n, send_s, recv_e, recv_w, recv_n, recv_s,
    mom_send, mom_y, mom_x_send, mom_x,
    edge_s, edge_n, edge_w, edge_e,
    ctl_send, ctl_x, ctl_y_send, ctl_y,
    hs, hr, ls, lr, mys, myr, mxs, mxr, cxs, cxr, cys, cyr,
):
    col = lax.axis_index("gx")
    row = lax.axis_index("gy")
    cy, cx = surface.shape
    pack = edge_s.shape[0]
    has = []
    for dx, dy in DIRS:
        ok = None
        for d, pos, size in ((dx, col, tiles_lon), (dy, row, tiles_lat)):
            if d:
                here = (pos < size - 1) if d > 0 else (pos > 0)
                ok = here if ok is None else ok & here
        has.append(ok)

    barrier = pltpu.get_barrier_semaphore()
    for d in range(1, tiles_lon):
        pl.semaphore_signal(barrier, inc=1, device_id=(lax.rem(col + d, tiles_lon), row), device_id_type=MESH)
    for d in range(1, tiles_lat):
        pl.semaphore_signal(barrier, inc=1, device_id=(col, lax.rem(row + d, tiles_lat)), device_id_type=MESH)
    for i in range(4, 8):
        dx, dy = DIRS[i]

        @pl.when(has[i])
        def _():
            pl.semaphore_signal(barrier, inc=1, device_id=(col + dx, row + dy), device_id_type=MESH)

    q_slots = [q_e, q_w, q_n, q_s] + [q_c.at[i] for i in range(4)]
    for i, slot in enumerate(q_slots):

        @pl.when(jnp.logical_not(has[i]))
        def _():
            slot[...] = jnp.zeros(slot.shape, F32)

    l_slots = [recv_e, recv_w, recv_n, recv_s]
    for i, slot in enumerate(l_slots):

        @pl.when(jnp.logical_not(has[i]))
        def _():
            slot[...] = jnp.zeros(slot.shape, F32)

    for buf in (send_e, send_w, send_n, send_s):
        buf[...] = jnp.zeros(buf.shape, F32)

    lane = lax.broadcasted_iota(jnp.int32, (cy, cx), 1)

    def forcing_level(k, acc):
        wet = mask[k].astype(F32)
        return acc + wet * (forcing[0, k] * tracer[0, k] + forcing[1, k] * tracer[1, k])

    rhs = lax.fori_loop(0, levels, forcing_level, surface[...])
    quad[0] = rhs
    quad[1] = cond_e[...]
    quad[2] = cond_n[...]
    quad[3] = diag[...]

    n_signals = tiles_lon - 1 + tiles_lat - 1
    total = jnp.int32(n_signals)
    for i in range(4, 8):
        total = total + has[i].astype(jnp.int32)
    pl.semaphore_wait(barrier, total)

    q_src = [
        quad, quad, quad.at[:, cy - 8 : cy, :], quad.at[:, 0:8, :],
        quad.at[:, cy - 8 : cy, :], quad.at[:, cy - 8 : cy, :],
        quad.at[:, 0:8, :], quad.at[:, 0:8, :],
    ]

    def q_copy(i):
        dx, dy = DIRS[i]
        o = OPPOSITE[i]
        return pltpu.make_async_remote_copy(
            src_ref=q_src[i], dst_ref=q_slots[o], send_sem=hs.at[i], recv_sem=hr.at[o],
            device_id=(col + dx, row + dy), device_id_type=MESH)

    def q_arrival(i):
        dx, dy = DIRS[i]
        return pltpu.make_async_remote_copy(
            src_ref=q_slots[i], dst_ref=q_slots[i], send_sem=hs.at[i], recv_sem=hr.at[i],
            device_id=(col + dx, row + dy), device_id_type=MESH)

    for i in range(8):

        @pl.when(has[i])
        def _():
            q_copy(i).start()

    def forward(k, kap, carry):
        kap_prev, ratio_prev, r0, r1, r2, r3 = carry
        wet = mask[k].astype(F32)
        inv = 1.0 / (1.0 + kap + kap_prev * (1.0 - ratio_prev))
        new_ratio = kap * inv
        r0 = (tracer[0, k] + kap_prev * r0) * inv
        r1 = (tracer[1, k] + kap_prev * r1) * inv
        r2 = (wet * load[0, k] + kap_prev * r2) * inv
        r3 = (wet * load[1, k] + kap_prev * r3) * inv
        ratio[k] = new_ratio
        red[0, k] = r0
        red[1, k] = r1
        red[2, k] = r2
        red[3, k] = r3
        packed = column_roll(flow_e[k], k + 1)
        send_e[2] = jnp.where(lane == k, packed, send_e[2])
        send_n[2, pl.ds(k, 1), :] = flow_n[k, cy - 1 : cy, :]
        return kap, new_ratio, r0, r1, r2, r3

    def forward_level(k, carry):
        return forward(k, mix[k] * mask[k + 1].astype(F32), carry)

    zero = jnp.zeros((cy, cx), F32)
    carry = lax.fori_loop(0, levels - 1, forward_level, (zero,) * 6)
    forward(levels - 1, zero, carry)

    for i in range(8):

        @pl.when(has[i])
        def _():
            q_arrival(i).wait_recv()

    lane8 = lax.broadcasted_iota(jnp.int32, (8, cx), 1) < cx // 2
    sub8 = lax.broadcasted_iota(jnp.int32, (8, cx), 0) < 4
    lane_half = lane < cx // 2

    def extend(f):
        side = jnp.where(lane_half, q_e[f], q_w[f])
        ends = jnp.where(sub8, q_n[f], q_s[f])
        corner = jnp.where(
            sub8, jnp.where(lane8, q_c[0, f], q_c[1, f]), jnp.where(lane8, q_c[2, f], q_c[3, f]))
        return jnp.concatenate(
            [jnp.concatenate([quad[f], ends], axis=0), jnp.concatenate([side, corner], axis=0)], axis=1)

    v0, ce, cn, dg = extend(0), extend(1), extend(2), extend(3)
    v1 = surface_apply(v0, ce, cn, dg)
    v2 = surface_apply(v1, ce, cn, dg)
    v3 = surface_apply(v2, ce, cn, dg)
    o0, o1, o2, o3 = (v[:cy, :cx] for v in (v0, v1, v2, v3))
    pairs = ((o0, o0), (o0, o1), (o1, o1), (o1, o2), (o2, o2), (o2, o3))
    mom_send[...] = jnp.concatenate(
        [jnp.sum(a * b, axis=0, keepdims=True) for a, b in pairs] + [jnp.zeros((2, cx), F32)], axis=0)

    def along_y(d, src, dst, ssem, rsem):
        return pltpu.make_async_remote_copy(
            src_ref=src, dst_ref=dst, send_sem=ssem.at[d - 1], recv_sem=rsem.at[d - 1],
            device_id=(col, lax.rem(row + d, tiles_lat)), device_id_type=MESH)

    def along_x(d, src, dst, ssem, rsem):
        return pltpu.make_async_remote_copy(
            src_ref=src, dst_ref=dst, send_sem=ssem.at[d - 1], recv_sem=rsem.at[d - 1],
            device_id=(lax.rem(col + d, tiles_lon), row), device_id_type=MESH)

    for d in range(1, tiles_lat):
        along_y(d, mom_send, mom_y.at[d - 1], mys, myr).start()

    def backward_level(step, carry):
        k = levels - 1 - step
        c = list(carry)
        wet = mask[k].astype(F32)
        rat = ratio[k]
        for f in range(4):
            c[f] = red[f, k] + rat * c[f]
            lam = wet * c[f]
            red[f, k] = lam
            kind, s = f // 2, f % 2
            idx = s * levels + k
            packed = column_roll(lam, idx + 1)
            send_e[kind] = jnp.where(lane == idx, packed, send_e[kind])
            send_w[kind] = jnp.where(lane == idx + 1, packed, send_w[kind])
            send_s[kind, pl.ds(idx, 1), :] = lam[0:1]
            send_n[kind, pl.ds(idx, 1), :] = lam[cy - 1 : cy]
        return tuple(c)

    lax.fori_loop(0, levels, backward_level, (zero,) * 4)

    l_src = [send_e, send_w, send_n, send_s]

    def l_copy(i):
        dx, dy = DIRS[i]
        o = OPPOSITE[i]
        return pltpu.make_async_remote_copy(
            src_ref=l_src[i], dst_ref=l_slots[o], send_sem=ls.at[i], recv_sem=lr.at[o],
            device_id=(col + dx, row + dy), device_id_type=MESH)

    def l_arrival(i):
        dx, dy = DIRS[i]
        return pltpu.make_async_remote_copy(
            src_ref=l_slots[i], dst_ref=l_slots[i], send_sem=ls.at[i], recv_sem=lr.at[i],
            device_id=(col + dx, row + dy), device_id_type=MESH)

    for i in range(4):

        @pl.when(has[i])
        def _():
            l_copy(i).start()

    part = mom_send[...]
    for d in range(1, tiles_lat):
        along_y(d, mom_send, mom_y.at[d - 1], mys, myr).wait_recv()
    for d in range(1, tiles_lat):
        part = part + mom_y[d - 1]
    mom_x_send[...] = part
    for d in range(1, tiles_lon):
        along_x(d, mom_x_send, mom_x.at[d - 1], mxs, mxr).start()
    for d in range(1, tiles_lon):
        along_x(d, mom_x_send, mom_x.at[d - 1], mxs, mxr).wait_recv()
    for d in range(1, tiles_lon):
        part = part + mom_x[d - 1]
    sums = jnp.sum(part, axis=1, keepdims=True)
    w0, w1, w2 = gradient_weights([sums[i : i + 1] for i in range(6)])
    x = w0 * v0 + w1 * v1 + w2 * v2
    x_own = x[:cy, :cx]
    surf_out[...] = x_own

    for i in range(4):

        @pl.when(has[i])
        def _():
            l_arrival(i).wait_recv()

    lam_e_cols = recv_e[0] + x[:cy, cx : cx + 1] * recv_e[1]
    lam_w_cols = recv_w[0] + x[:cy, 2 * cx - 1 : 2 * cx] * recv_w[1]
    recv_n[0] = recv_n[0] + x[cy : cy + 1, :cx] * recv_n[1]
    recv_s[0] = recv_s[0] + x[cy + 7 : cy + 8, :cx] * recv_s[1]

    edge_w[...] = jnp.zeros(edge_w.shape, F32)
    edge_e[...] = jnp.zeros(edge_e.shape, F32)
    edge_s[...] = jnp.zeros(edge_s.shape, F32)
    edge_n[...] = jnp.zeros(edge_n.shape, F32)
    sub = lax.broadcasted_iota(jnp.int32, (cy, cx), 0)
    first_lane, last_lane = lane == 0, lane == cx - 1
    first_row, last_row = sub == 0, sub == cy - 1

    def final_level(k, carry):
        half_e = 0.5 * flow_e[k]
        half_n = 0.5 * flow_n[k]
        half_w_halo = 0.5 * column_roll(recv_w[2], cx - k)
        half_s_halo = 0.5 * recv_s[2, pl.ds(k, 1), :]
        for s in range(2):
            idx = s * levels + k
            lam = red[s, k] + x_own * red[2 + s, k]
            lam_e = jnp.where(last_lane, column_roll(lam_e_cols, cx - 2 - idx), column_roll(lam, cx - 1))
            lam_n = jnp.where(last_row, recv_n[0, pl.ds(idx, 1), :], pltpu.roll(lam, cy - 1, 0))
            flux_e = half_e * (lam_e - lam)
            flux_n = half_n * (lam_n - lam)
            halo_w = half_w_halo * (lam - column_roll(lam_w_cols, cx - idx))
            halo_s = half_s_halo * (lam[0:1] - recv_s[0, pl.ds(idx, 1), :])
            flux_w = jnp.where(first_lane, halo_w, column_roll(flux_e, 1))
            flux_s = jnp.where(first_row, halo_s, pltpu.roll(flux_n, 1, 0))
            g = lam + flux_e + flux_w + flux_n + flux_s
            grad_out[s, k] = g
            packed = column_roll(g, idx + 1)
            edge_e[0:cy] = jnp.where(lane == idx, packed, edge_e[0:cy])
            edge_w[0:cy] = jnp.where(lane == idx + 1, packed, edge_w[0:cy])
            edge_s[pl.ds(idx, 1), :] = g[0:1]
            edge_n[pl.ds(idx, 1), :] = g[cy - 1 : cy]
        return carry

    lax.fori_loop(0, levels, final_level, 0)

    lon, lat = tiles_lon * cx, tiles_lat * cy
    controls = ctl_send.shape[0]
    lane_row = lax.broadcasted_iota(jnp.int32, (1, LANES), 1)
    last_chunk = cmap.shape[0] - 1

    def points(ref, begin):
        chunk = begin // LANES
        off = lax.rem(begin, LANES)
        near = ref[pl.ds(chunk, 1), :]
        far = ref[pl.ds(jnp.minimum(chunk + 1, last_chunk), 1), :]
        back = lax.rem(LANES - off, LANES)
        return jnp.where(
            lane_row < LANES - off, pltpu.roll(near, back, 1), pltpu.roll(far, back, 1))

    control_ids = lax.broadcasted_iota(jnp.int32, (controls, LANES), 0)
    sides = (
        (col * cx, cx, row == 0, edge_s, True),
        (lon + col * cx, cx, row == tiles_lat - 1, edge_n, True),
        (2 * lon + row * cy, cy, col == 0, edge_w, False),
        (2 * lon + lat + row * cy, cy, col == tiles_lon - 1, edge_e, False),
    )
    ctl_send[...] = jnp.zeros(ctl_send.shape, F32)
    for begin, count, active, edge, by_rows in sides:

        @pl.when(active)
        def _():
            ids = points(cmap, begin)
            wts = jnp.where(lane_row < count, points(cwt, begin), 0.0)
            spread = jnp.where(control_ids == ids, wts, 0.0)
            values = edge[...]
            if edge is edge_w:
                values = column_roll(values, LANES - 1)
            dims = (((1,), (1,)), ((), ())) if by_rows else (((1,), (0,)), ((), ()))
            ctl_send[...] += lax.dot_general(
                spread, values, dims, precision=HIGHEST, preferred_element_type=F32)

    share = controls // tiles_lon
    for d in range(1, tiles_lon):
        begin = pl.multiple_of(lax.rem(col + d, tiles_lon) * share, 8)
        along_x(d, ctl_send.at[pl.ds(begin, share), :], ctl_x.at[d - 1], cxs, cxr).start()
    mine = ctl_send[pl.ds(pl.multiple_of(col * share, 8), share), :]
    for d in range(1, tiles_lon):
        along_x(d, ctl_send.at[pl.ds(0, share), :], ctl_x.at[d - 1], cxs, cxr).wait_recv()
    for d in range(1, tiles_lon):
        mine = mine + ctl_x[d - 1]
    ctl_y_send[...] = jnp.zeros(ctl_y_send.shape, F32)
    for j in range(tiles_lat):
        ctl_y_send[j, 0:CTRL_DEV] = mine[j * CTRL_DEV : (j + 1) * CTRL_DEV]
    for d in range(1, tiles_lat):
        along_y(d, ctl_y_send.at[lax.rem(row + d, tiles_lat)], ctl_y.at[d - 1], cys, cyr).start()
    result = ctl_y_send[row]
    for d in range(1, tiles_lat):
        along_y(d, ctl_y_send.at[0], ctl_y.at[d - 1], cys, cyr).wait_recv()
    for d in range(1, tiles_lat):
        result = result + ctl_y[d - 1]
    turned = jnp.concatenate([result, jnp.zeros((LANES - SLOT, LANES), F32)], axis=0).T
    for s in range(2):
        ctrl_out[s] = turned[s * levels : (s + 1) * levels, 0:CTRL_DEV]

    for i in range(8):

        @pl.when(has[i])
        def _():
            q_copy(i).wait_send()

    for i in range(4):

        @pl.when(has[i])
        def _():
            l_copy(i).wait_send()

    for d in range(1, tiles_lat):
        along_y(d, mom_send, mom_y.at[d - 1], mys, myr).wait_send()
        along_y(d, ctl_y_send.at[0], ctl_y.at[d - 1], cys, cyr).wait_send()
    for d in range(1, tiles_lon):
        along_x(d, mom_x_send, mom_x.at[d - 1], mxs, mxr).wait_send()
        along_x(d, ctl_send.at[pl.ds(0, share), :], ctl_x.at[d - 1], cxs, cxr).wait_send()


def per_device(
    tracer_adjoint, surface_adjoint, flow_east, flow_north, vertical_mix, land_mask,
    conduct_east, conduct_north, surface_diagonal, pressure_load, surface_forcing,
    control_map, control_weight,
):
    tiles_lon, tiles_lat = lax.axis_size("gx"), lax.axis_size("gy")
    _, levels, cy, cx = tracer_adjoint.shape
    pack = -(-2 * levels // 8) * 8
    controls = CTRL_DEV * tiles_lon * tiles_lat
    vmem = pl.BlockSpec(memory_space=pltpu.VMEM)
    smem = pl.BlockSpec(memory_space=pltpu.SMEM)
    dma = pltpu.SemaphoreType.DMA
    buf = lambda *shape: pltpu.VMEM(shape, F32)
    scratch = [
        buf(4, levels, cy, cx), buf(levels, cy, cx), buf(4, cy, cx),
        buf(4, cy, cx), buf(4, cy, cx), buf(4, 8, cx), buf(4, 8, cx), buf(4, 4, 8, cx),
        buf(3, cy, cx), buf(2, cy, cx), buf(3, pack, cx), buf(2, pack, cx),
        buf(2, cy, cx), buf(3, cy, cx), buf(2, pack, cx), buf(3, pack, cx),
        buf(8, cx), buf(tiles_lat - 1, 8, cx), buf(8, cx), buf(tiles_lon - 1, 8, cx),
        buf(LANES, cx), buf(LANES, cx), buf(LANES, cx), buf(LANES, cx),
        buf(controls, LANES), buf(tiles_lon - 1, controls // tiles_lon, LANES),
        buf(tiles_lat, SLOT, LANES), buf(tiles_lat - 1, SLOT, LANES),
        dma((8,)), dma((8,)), dma((4,)), dma((4,)),
        dma((tiles_lat - 1,)), dma((tiles_lat - 1,)), dma((tiles_lon - 1,)), dma((tiles_lon - 1,)),
        dma((tiles_lon - 1,)), dma((tiles_lon - 1,)), dma((tiles_lat - 1,)), dma((tiles_lat - 1,)),
    ]
    return pl.pallas_call(
        functools.partial(step_kernel, tiles_lon, tiles_lat, levels),
        out_shape=(
            jax.ShapeDtypeStruct(tracer_adjoint.shape, F32),
            jax.ShapeDtypeStruct(surface_adjoint.shape, F32),
            jax.ShapeDtypeStruct((2, levels, CTRL_DEV), F32),
        ),
        in_specs=[vmem] * 9 + [smem] * 2 + [vmem] * 2,
        out_specs=(vmem, vmem, vmem),
        scratch_shapes=scratch,
        compiler_params=pltpu.CompilerParams(
            collective_id=0, has_side_effects=True, vmem_limit_bytes=48 * 1024 * 1024),
    )(
        tracer_adjoint, surface_adjoint, flow_east, flow_north, vertical_mix, land_mask,
        conduct_east, conduct_north, surface_diagonal, pressure_load, surface_forcing,
        control_map.reshape(-1, LANES), control_weight.reshape(-1, LANES),
    )


def solution(mesh):
    in_specs = (
        P(None, None, "gy", "gx"), P("gy", "gx"),
        P(None, "gy", "gx"), P(None, "gy", "gx"), P(None, "gy", "gx"), P(None, "gy", "gx"),
        P("gy", "gx"), P("gy", "gx"), P("gy", "gx"), P(), P(), P(), P(),
    )
    out_specs = (P(None, None, "gy", "gx"), P("gy", "gx"), P(None, None, ("gx", "gy")))
    return jax.shard_map(
        per_device, mesh=mesh, in_specs=in_specs, out_specs=out_specs, check_vma=False
    )
```

```python
import functools
import jax
import jax.numpy as jnp
from jax import lax
from jax.experimental import pallas as pl
from jax.experimental.pallas import tpu as pltpu
from jax.sharding import PartitionSpec as P

ITERS = 3
CTRL_DEV = 10
SLOT = 16
VMEM_LIMIT = 63_200 * 1024
LANES = 128
MESH = pl.DeviceIdType.MESH
DIRS = ((1, 0), (-1, 0), (0, 1), (0, -1), (1, 1), (-1, 1), (1, -1), (-1, -1))
OPPOSITE = (1, 0, 3, 2, 7, 6, 5, 4)
F32 = jnp.float32
HIGHEST = lax.Precision.HIGHEST


def unrolled(count, body, carry):
    width = max(u for u in range(1, 8) if count % u == 0)

    def several(i, carry):
        for u in range(width):
            carry = body(i * width + u, carry)
        return carry

    return lax.fori_loop(0, count // width, several, carry)


def column_roll(value, shift):
    return pltpu.roll(value, shift, 1)


def surface_apply(e, ce, cn, dg):
    rows, cols = e.shape
    flux_e = ce * (e - pltpu.roll(e, cols - 1, 1))
    flux_n = cn * (e - pltpu.roll(e, rows - 1, 0))
    return dg * e + (flux_e - pltpu.roll(flux_e, 1, 1)) + (flux_n - pltpu.roll(flux_n, 1, 0))


def poly_add(p, q, factor):
    size = max(len(p), len(q))
    out = []
    for i in range(size):
        term = factor * q[i] if i < len(q) else None
        if i < len(p):
            term = p[i] if term is None else p[i] + term
        out.append(term)
    return out


def gradient_weights(mu):
    def inner(p, q, shift):
        total = None
        for i, pi in enumerate(p):
            for j, qj in enumerate(q):
                term = pi * qj * mu[i + j + shift]
                total = term if total is None else total + term
        return total

    one = jnp.ones_like(mu[0])
    zero = jnp.zeros_like(mu[0])
    floor = 2e-7 * mu[0]
    res, search, x = [one], [one], [zero]
    rr = mu[0]
    for it in range(ITERS):
        den = inner(search, search, 1)
        good = (den > 0) & (rr > floor)
        step = jnp.where(good, rr / jnp.where(good, den, one), zero)
        x = poly_add(x, search, step)
        if it + 1 < ITERS:
            res = poly_add(res, [zero] + search, -step)
            rr_new = jnp.maximum(inner(res, res, 0), zero)
            ratio = jnp.where(good, rr_new / jnp.where(good, rr, one), zero)
            search = poly_add(res, search, ratio)
            rr = rr_new
    return x


def step_kernel(
    tiles_lon, tiles_lat, levels,
    tracer_in, surface_in, flow_e_in, flow_n_in, mix_in, mask_in, cond_e_in, cond_n_in, diag_in,
    load_in, forcing_in, cmap_in, cwt_in,
    grad_out, surf_out, ctrl_out,
    tracer, surface, flow_e, flow_n, mix, mask, load, forcing, cmap, cwt, ins,
    red, ratio, quad, q_e, q_w, q_n, q_s, q_c,
    pk, send_n, send_s, recv_e, recv_w, recv_n, recv_s,
    mom_send, mom_y, mom_x_send, mom_x,
    edge_s, edge_n, edge_ew,
    ctl_send, ctl_x, ctl_y_send, ctl_y,
    hs, hr, ls, lr, mys, myr, mxs, mxr, cxs, cxr, cys, cyr,
):
    col = lax.axis_index("gx")
    row = lax.axis_index("gy")
    cy, cx = surface.shape
    moves = [
        pltpu.make_async_copy(src, dst, ins.at[i])
        for i, (src, dst) in enumerate((
            (forcing_in, forcing), (mask_in, mask), (tracer_in, tracer), (surface_in, surface),
            (cond_e_in, quad.at[1]), (cond_n_in, quad.at[2]), (diag_in, quad.at[3]),
            (load_in, load), (mix_in, mix), (flow_e_in, flow_e), (flow_n_in, flow_n),
            (cmap_in, cmap), (cwt_in, cwt)))
    ]
    for move in moves:
        move.start()
    has = []
    for dx, dy in DIRS:
        ok = None
        for d, pos, size in ((dx, col, tiles_lon), (dy, row, tiles_lat)):
            if d:
                here = (pos < size - 1) if d > 0 else (pos > 0)
                ok = here if ok is None else ok & here
        has.append(ok)

    barrier = pltpu.get_barrier_semaphore()
    for d in range(1, tiles_lon):
        pl.semaphore_signal(barrier, inc=1, device_id=(lax.rem(col + d, tiles_lon), row), device_id_type=MESH)
    for d in range(1, tiles_lat):
        pl.semaphore_signal(barrier, inc=1, device_id=(col, lax.rem(row + d, tiles_lat)), device_id_type=MESH)
    for i in range(4, 8):
        dx, dy = DIRS[i]

        @pl.when(has[i])
        def _():
            pl.semaphore_signal(barrier, inc=1, device_id=(col + dx, row + dy), device_id_type=MESH)

    q_slots = [q_e, q_w, q_n, q_s] + [q_c.at[i] for i in range(4)]
    for i, slot in enumerate(q_slots):

        @pl.when(jnp.logical_not(has[i]))
        def _():
            slot[...] = jnp.zeros(slot.shape, F32)

    l_slots = [recv_e, recv_w, recv_n, recv_s]
    for i, slot in enumerate(l_slots):

        @pl.when(jnp.logical_not(has[i]))
        def _():
            slot[...] = jnp.zeros(slot.shape, F32)

    for buf in (pk, send_n, send_s, edge_s, edge_n, edge_ew):
        buf[...] = jnp.zeros(buf.shape, F32)

    for move in moves[:4]:
        move.wait()

    lane = lax.broadcasted_iota(jnp.int32, (cy, cx), 1)

    def forcing_level(k, acc):
        wet = mask[k].astype(F32)
        return acc + wet * (forcing[0, k] * tracer[0, k] + forcing[1, k] * tracer[1, k])

    quad[0] = unrolled(levels, forcing_level, surface[...])
    for move in moves[4:7]:
        move.wait()

    n_signals = tiles_lon - 1 + tiles_lat - 1
    total = jnp.int32(n_signals)
    for i in range(4, 8):
        total = total + has[i].astype(jnp.int32)
    pl.semaphore_wait(barrier, total)

    q_src = [
        quad, quad, quad.at[:, cy - 8 : cy, :], quad.at[:, 0:8, :],
        quad.at[:, cy - 8 : cy, :], quad.at[:, cy - 8 : cy, :],
        quad.at[:, 0:8, :], quad.at[:, 0:8, :],
    ]

    def q_copy(i):
        dx, dy = DIRS[i]
        o = OPPOSITE[i]
        return pltpu.make_async_remote_copy(
            src_ref=q_src[i], dst_ref=q_slots[o], send_sem=hs.at[i], recv_sem=hr.at[o],
            device_id=(col + dx, row + dy), device_id_type=MESH)

    def q_arrival(i):
        dx, dy = DIRS[i]
        return pltpu.make_async_remote_copy(
            src_ref=q_slots[i], dst_ref=q_slots[i], send_sem=hs.at[i], recv_sem=hr.at[i],
            device_id=(col + dx, row + dy), device_id_type=MESH)

    for i in range(8):

        @pl.when(has[i])
        def _():
            q_copy(i).start()

    def forward(k, kap, carry):
        kap_prev, ratio_prev, r0, r1, r2, r3 = carry
        wet = mask[k].astype(F32)
        inv = 1.0 / (1.0 + kap + kap_prev * (1.0 - ratio_prev))
        new_ratio = kap * inv
        r0 = (tracer[0, k] + kap_prev * r0) * inv
        r1 = (tracer[1, k] + kap_prev * r1) * inv
        r2 = (wet * load[0, k] + kap_prev * r2) * inv
        r3 = (wet * load[1, k] + kap_prev * r3) * inv
        ratio[k] = new_ratio
        red[0, k] = r0
        red[1, k] = r1
        red[2, k] = r2
        red[3, k] = r3
        pk[4] = jnp.where(pair == k, column_roll(flow_e[k], 2 * k + 1), pk[4])
        send_n[2, pl.ds(k, 1), :] = flow_n[k, cy - 1 : cy, :]
        return kap, new_ratio, r0, r1, r2, r3

    def forward_level(k, carry):
        return forward(k, mix[k] * mask[k + 1].astype(F32), carry)

    for move in moves[7:11]:
        move.wait()
    pair = lane // 2
    zero = jnp.zeros((cy, cx), F32)
    carry = unrolled(levels - 1, forward_level, (zero,) * 6)
    forward(levels - 1, zero, carry)

    for i in range(8):

        @pl.when(has[i])
        def _():
            q_arrival(i).wait_recv()

    lane8 = lax.broadcasted_iota(jnp.int32, (8, cx), 1) < cx // 2
    sub8 = lax.broadcasted_iota(jnp.int32, (8, cx), 0) < 4
    lane_half = lane < cx // 2

    def extend(f):
        side = jnp.where(lane_half, q_e[f], q_w[f])
        ends = jnp.where(sub8, q_n[f], q_s[f])
        corner = jnp.where(
            sub8, jnp.where(lane8, q_c[0, f], q_c[1, f]), jnp.where(lane8, q_c[2, f], q_c[3, f]))
        return jnp.concatenate(
            [jnp.concatenate([quad[f], ends], axis=0), jnp.concatenate([side, corner], axis=0)], axis=1)

    v0, ce, cn, dg = extend(0), extend(1), extend(2), extend(3)
    v1 = surface_apply(v0, ce, cn, dg)
    v2 = surface_apply(v1, ce, cn, dg)
    v3 = surface_apply(v2, ce, cn, dg)
    o0, o1, o2, o3 = (v[:cy, :cx] for v in (v0, v1, v2, v3))
    pairs = ((o0, o0), (o0, o1), (o1, o1), (o1, o2), (o2, o2), (o2, o3))
    mom_send[...] = jnp.concatenate(
        [jnp.sum(a * b, axis=0, keepdims=True) for a, b in pairs] + [jnp.zeros((2, cx), F32)], axis=0)

    def along_y(d, src, dst, ssem, rsem):
        return pltpu.make_async_remote_copy(
            src_ref=src, dst_ref=dst, send_sem=ssem.at[d - 1], recv_sem=rsem.at[d - 1],
            device_id=(col, lax.rem(row + d, tiles_lat)), device_id_type=MESH)

    def along_x(d, src, dst, ssem, rsem):
        return pltpu.make_async_remote_copy(
            src_ref=src, dst_ref=dst, send_sem=ssem.at[d - 1], recv_sem=rsem.at[d - 1],
            device_id=(lax.rem(col + d, tiles_lon), row), device_id_type=MESH)

    for d in range(1, tiles_lat):
        along_y(d, mom_send, mom_y.at[d - 1], mys, myr).start()

    def backward_level(step, carry):
        k = levels - 1 - step
        c = list(carry)
        wet = mask[k].astype(F32)
        rat = ratio[k]
        for f in range(4):
            c[f] = red[f, k] + rat * c[f]
            lam = wet * c[f]
            red[f, k] = lam
            kind, s = f // 2, f % 2
            idx = s * levels + k
            pk[f] = jnp.where(pair == k, column_roll(lam, 2 * k + 1), pk[f])
            send_s[kind, pl.ds(idx, 1), :] = lam[0:1]
            send_n[kind, pl.ds(idx, 1), :] = lam[cy - 1 : cy]
        return tuple(c)

    unrolled(levels, backward_level, (zero,) * 4)

    l_src = [pk, pk.at[0:4], send_n, send_s]

    def l_copy(i):
        dx, dy = DIRS[i]
        o = OPPOSITE[i]
        return pltpu.make_async_remote_copy(
            src_ref=l_src[i], dst_ref=l_slots[o], send_sem=ls.at[i], recv_sem=lr.at[o],
            device_id=(col + dx, row + dy), device_id_type=MESH)

    def l_arrival(i):
        dx, dy = DIRS[i]
        return pltpu.make_async_remote_copy(
            src_ref=l_slots[i], dst_ref=l_slots[i], send_sem=ls.at[i], recv_sem=lr.at[i],
            device_id=(col + dx, row + dy), device_id_type=MESH)

    for i in range(4):

        @pl.when(has[i])
        def _():
            l_copy(i).start()

    part = mom_send[...]
    for d in range(1, tiles_lat):
        along_y(d, mom_send, mom_y.at[d - 1], mys, myr).wait_recv()
    for d in range(1, tiles_lat):
        part = part + mom_y[d - 1]
    mom_x_send[...] = part
    for d in range(1, tiles_lon):
        along_x(d, mom_x_send, mom_x.at[d - 1], mxs, mxr).start()
    for d in range(1, tiles_lon):
        along_x(d, mom_x_send, mom_x.at[d - 1], mxs, mxr).wait_recv()
    for d in range(1, tiles_lon):
        part = part + mom_x[d - 1]
    sums = jnp.sum(part, axis=1, keepdims=True)
    w0, w1, w2 = gradient_weights([sums[i : i + 1] for i in range(6)])
    x = w0 * v0 + w1 * v1 + w2 * v2
    x_own = x[:cy, :cx]
    surf_out[...] = x_own

    for i in range(4):

        @pl.when(has[i])
        def _():
            l_arrival(i).wait_recv()

    even = lane == 2 * pair
    x_e, x_w = x[:cy, cx : cx + 1], x[:cy, 2 * cx - 1 : 2 * cx]
    for s in range(2):
        recv_e[s] = jnp.where(
            even,
            column_roll(recv_e[s] + x_e * recv_e[2 + s], cx - 1),
            column_roll(recv_w[s] + x_w * recv_w[2 + s], 1))
    recv_n[0] = recv_n[0] + x[cy : cy + 1, :cx] * recv_n[1]
    recv_s[0] = recv_s[0] + x[cy + 7 : cy + 8, :cx] * recv_s[1]

    sub = lax.broadcasted_iota(jnp.int32, (cy, cx), 0)
    first_lane, last_lane = lane == 0, lane == cx - 1
    first_row, last_row = sub == 0, sub == cy - 1

    def final_level(k, carry):
        half_e = 0.5 * flow_e[k]
        half_n = 0.5 * flow_n[k]
        half_w_halo = 0.5 * column_roll(recv_w[4], lax.rem(cx - 2 * k, cx))
        half_s_halo = 0.5 * recv_s[2, pl.ds(k, 1), :]
        for s in range(2):
            idx = s * levels + k
            lam = red[s, k] + x_own * red[2 + s, k]
            side = column_roll(recv_e[s], cx - 1 - 2 * k)
            lam_e = jnp.where(last_lane, side, column_roll(lam, cx - 1))
            lam_n = jnp.where(last_row, recv_n[0, pl.ds(idx, 1), :], pltpu.roll(lam, cy - 1, 0))
            flux_e = half_e * (lam_e - lam)
            flux_n = half_n * (lam_n - lam)
            halo_w = half_w_halo * (lam - side)
            halo_s = half_s_halo * (lam[0:1] - recv_s[0, pl.ds(idx, 1), :])
            flux_w = jnp.where(first_lane, halo_w, column_roll(flux_e, 1))
            flux_s = jnp.where(first_row, halo_s, pltpu.roll(flux_n, 1, 0))
            g = lam + flux_e + flux_w + flux_n + flux_s
            grad_out[s, k] = g
            edge_ew[s] = jnp.where(pair == k, column_roll(g, 2 * k + 1), edge_ew[s])
            edge_s[pl.ds(idx, 1), :] = g[0:1]
            edge_n[pl.ds(idx, 1), :] = g[cy - 1 : cy]
        return carry

    unrolled(levels, final_level, 0)
    for move in moves[11:]:
        move.wait()

    lon, lat = tiles_lon * cx, tiles_lat * cy
    controls = ctl_send.shape[0]
    lane_row = lax.broadcasted_iota(jnp.int32, (1, LANES), 1)
    last_chunk = cmap.shape[0] - 1

    def points(ref, begin):
        chunk = begin // LANES
        off = lax.rem(begin, LANES)
        near = ref[pl.ds(chunk, 1), :]
        far = ref[pl.ds(jnp.minimum(chunk + 1, last_chunk), 1), :]
        back = lax.rem(LANES - off, LANES)
        return jnp.where(
            lane_row < LANES - off, pltpu.roll(near, back, 1), pltpu.roll(far, back, 1))

    control_ids = lax.broadcasted_iota(jnp.int32, (controls, LANES), 0)
    sides = (
        (col * cx, cx, row == 0, edge_s, None),
        (lon + col * cx, cx, row == tiles_lat - 1, edge_n, None),
        (2 * lon + row * cy, cy, col == 0, edge_ew, 1),
        (2 * lon + lat + row * cy, cy, col == tiles_lon - 1, edge_ew, 0),
    )
    ctl_send[...] = jnp.zeros(ctl_send.shape, F32)
    for begin, count, active, edge, odd in sides:

        @pl.when(active)
        def _():
            ids = points(cmap, begin)
            wts = jnp.where(lane_row < count, points(cwt, begin), 0.0)
            spread = jnp.where(control_ids == ids, wts, 0.0)
            if odd is None:
                values, dims = edge[...], (((1,), (1,)), ((), ()))
            else:
                source = lax.broadcasted_iota(jnp.int32, (LANES, LANES), 0)
                target = lax.broadcasted_iota(jnp.int32, (LANES, LANES), 1)
                values, dims = jnp.zeros((cy, LANES), F32), (((1,), (0,)), ((), ()))
                for s in range(2):
                    level = target - s * levels
                    move = (source == 2 * level + odd) & (level >= 0) & (level < levels)
                    values += lax.dot_general(
                        edge[s], move.astype(F32), dims, precision=HIGHEST,
                        preferred_element_type=F32)
                spread = spread[:, :cy]
            ctl_send[...] += lax.dot_general(
                spread, values, dims, precision=HIGHEST, preferred_element_type=F32)

    share = controls // tiles_lon
    for d in range(1, tiles_lon):
        begin = pl.multiple_of(lax.rem(col + d, tiles_lon) * share, 8)
        along_x(d, ctl_send.at[pl.ds(begin, share), :], ctl_x.at[d - 1], cxs, cxr).start()
    mine = ctl_send[pl.ds(pl.multiple_of(col * share, 8), share), :]
    for d in range(1, tiles_lon):
        along_x(d, ctl_send.at[pl.ds(0, share), :], ctl_x.at[d - 1], cxs, cxr).wait_recv()
    for d in range(1, tiles_lon):
        mine = mine + ctl_x[d - 1]
    ctl_y_send[...] = jnp.zeros(ctl_y_send.shape, F32)
    for j in range(tiles_lat):
        ctl_y_send[j, 0:CTRL_DEV] = mine[j * CTRL_DEV : (j + 1) * CTRL_DEV]
    for d in range(1, tiles_lat):
        along_y(d, ctl_y_send.at[lax.rem(row + d, tiles_lat)], ctl_y.at[d - 1], cys, cyr).start()
    result = ctl_y_send[row]
    for d in range(1, tiles_lat):
        along_y(d, ctl_y_send.at[0], ctl_y.at[d - 1], cys, cyr).wait_recv()
    for d in range(1, tiles_lat):
        result = result + ctl_y[d - 1]
    for s in range(2):
        ctrl_out[:, s, :] = result[0:CTRL_DEV, s * levels : (s + 1) * levels]

    for i in range(8):

        @pl.when(has[i])
        def _():
            q_copy(i).wait_send()

    for i in range(4):

        @pl.when(has[i])
        def _():
            l_copy(i).wait_send()

    for d in range(1, tiles_lat):
        along_y(d, mom_send, mom_y.at[d - 1], mys, myr).wait_send()
        along_y(d, ctl_y_send.at[0], ctl_y.at[d - 1], cys, cyr).wait_send()
    for d in range(1, tiles_lon):
        along_x(d, mom_x_send, mom_x.at[d - 1], mxs, mxr).wait_send()
        along_x(d, ctl_send.at[pl.ds(0, share), :], ctl_x.at[d - 1], cxs, cxr).wait_send()


def results_kernel(grad, surf, ctrl, grad_out, surf_out, ctrl_out, sems):
    moves = [
        pltpu.make_async_copy(src, dst, sems.at[i])
        for i, (src, dst) in enumerate(((grad, grad_out), (surf, surf_out), (ctrl, ctrl_out)))
    ]
    for move in moves:
        move.start()
    for move in moves:
        move.wait()


def per_device(
    tracer_adjoint, surface_adjoint, flow_east, flow_north, vertical_mix, land_mask,
    conduct_east, conduct_north, surface_diagonal, pressure_load, surface_forcing,
    control_map, control_weight,
):
    tiles_lon, tiles_lat = lax.axis_size("gx"), lax.axis_size("gy")
    _, levels, cy, cx = tracer_adjoint.shape
    pack = -(-2 * levels // 8) * 8
    controls = CTRL_DEV * tiles_lon * tiles_lat
    points = control_map.shape[0]
    vmem = pl.BlockSpec(memory_space=pltpu.VMEM)
    hbm = pl.BlockSpec(memory_space=pltpu.HBM)
    dma = pltpu.SemaphoreType.DMA
    buf = lambda *shape: pltpu.VMEM(shape, F32)
    scratch = [
        buf(2, levels, cy, cx), buf(cy, cx), buf(levels, cy, cx), buf(levels, cy, cx),
        buf(levels - 1, cy, cx), pltpu.VMEM((levels, cy, cx), jnp.int32),
        pltpu.SMEM((2, levels), F32), pltpu.SMEM((2, levels), F32),
        pltpu.VMEM((points // LANES, LANES), jnp.int32), buf(points // LANES, LANES), dma((13,)),
        buf(4, levels, cy, cx), buf(levels, cy, cx), buf(4, cy, cx),
        buf(4, cy, cx), buf(4, cy, cx), buf(4, 8, cx), buf(4, 8, cx), buf(4, 4, 8, cx),
        buf(5, cy, cx), buf(3, pack, cx), buf(2, pack, cx),
        buf(4, cy, cx), buf(5, cy, cx), buf(2, pack, cx), buf(3, pack, cx),
        buf(8, cx), buf(tiles_lat - 1, 8, cx), buf(8, cx), buf(tiles_lon - 1, 8, cx),
        buf(LANES, cx), buf(LANES, cx), buf(2, cy, cx),
        buf(controls, LANES), buf(tiles_lon - 1, controls // tiles_lon, LANES),
        buf(tiles_lat, SLOT, LANES), buf(tiles_lat - 1, SLOT, LANES),
        dma((8,)), dma((8,)), dma((4,)), dma((4,)),
        dma((tiles_lat - 1,)), dma((tiles_lat - 1,)), dma((tiles_lon - 1,)), dma((tiles_lon - 1,)),
        dma((tiles_lon - 1,)), dma((tiles_lon - 1,)), dma((tiles_lat - 1,)), dma((tiles_lat - 1,)),
    ]
    grad, surf, ctrl = pl.pallas_call(
        functools.partial(step_kernel, tiles_lon, tiles_lat, levels),
        out_shape=(
            pltpu.VMEM(tracer_adjoint.shape, F32),
            pltpu.VMEM(surface_adjoint.shape, F32),
            pltpu.VMEM((CTRL_DEV, 2, levels), F32),
        ),
        in_specs=[hbm] * 13,
        out_specs=(vmem, vmem, vmem),
        scratch_shapes=scratch,
        compiler_params=pltpu.CompilerParams(
            collective_id=0, has_side_effects=True, vmem_limit_bytes=VMEM_LIMIT),
    )(
        tracer_adjoint, surface_adjoint, flow_east, flow_north, vertical_mix, land_mask,
        conduct_east, conduct_north, surface_diagonal, pressure_load, surface_forcing,
        control_map.reshape(-1, LANES), control_weight.reshape(-1, LANES),
    )
    grad, surf, ctrl = pl.pallas_call(
        results_kernel,
        out_shape=tuple(jax.ShapeDtypeStruct(a.shape, F32) for a in (grad, surf, ctrl)),
        in_specs=[vmem] * 3,
        out_specs=(hbm, hbm, hbm),
        scratch_shapes=[dma((3,))],
    )(grad, surf, ctrl)
    return grad, surf, ctrl.transpose(1, 2, 0)


def solution(mesh):
    in_specs = (
        P(None, None, "gy", "gx"), P("gy", "gx"),
        P(None, "gy", "gx"), P(None, "gy", "gx"), P(None, "gy", "gx"), P(None, "gy", "gx"),
        P("gy", "gx"), P("gy", "gx"), P("gy", "gx"), P(), P(), P(), P(),
    )
    out_specs = (P(None, None, "gy", "gx"), P("gy", "gx"), P(None, None, ("gx", "gy")))
    return jax.shard_map(
        per_device, mesh=mesh, in_specs=in_specs, out_specs=out_specs, check_vma=False
    )
```

```python
import functools
import jax
import jax.numpy as jnp
from jax import lax
from jax.experimental import pallas as pl
from jax.experimental.pallas import tpu as pltpu
from jax.sharding import PartitionSpec as P

ITERS = 3
CTRL_DEV = 10
SLOT = 16
VMEM_LIMIT = 63_200 * 1024
LANES = 128
MESH = pl.DeviceIdType.MESH
DIRS = ((1, 0), (-1, 0), (0, 1), (0, -1), (1, 1), (-1, 1), (1, -1), (-1, -1))
OPPOSITE = (1, 0, 3, 2, 7, 6, 5, 4)
F32 = jnp.float32
HIGHEST = lax.Precision.HIGHEST


def unrolled(count, body, carry):
    width = max(u for u in range(1, 8) if count % u == 0)

    def several(i, carry):
        for u in range(width):
            carry = body(i * width + u, carry)
        return carry

    return lax.fori_loop(0, count // width, several, carry)


def column_roll(value, shift):
    return pltpu.roll(value, shift, 1)


def surface_apply(e, ce, cn, dg):
    rows, cols = e.shape
    flux_e = ce * (e - pltpu.roll(e, cols - 1, 1))
    flux_n = cn * (e - pltpu.roll(e, rows - 1, 0))
    return dg * e + (flux_e - pltpu.roll(flux_e, 1, 1)) + (flux_n - pltpu.roll(flux_n, 1, 0))


def poly_add(p, q, factor):
    size = max(len(p), len(q))
    out = []
    for i in range(size):
        term = factor * q[i] if i < len(q) else None
        if i < len(p):
            term = p[i] if term is None else p[i] + term
        out.append(term)
    return out


def gradient_weights(mu):
    def inner(p, q, shift):
        total = None
        for i, pi in enumerate(p):
            for j, qj in enumerate(q):
                term = pi * qj * mu[i + j + shift]
                total = term if total is None else total + term
        return total

    one = jnp.ones_like(mu[0])
    zero = jnp.zeros_like(mu[0])
    floor = 2e-7 * mu[0]
    res, search, x = [one], [one], [zero]
    rr = mu[0]
    for it in range(ITERS):
        den = inner(search, search, 1)
        good = (den > 0) & (rr > floor)
        step = jnp.where(good, rr / jnp.where(good, den, one), zero)
        x = poly_add(x, search, step)
        if it + 1 < ITERS:
            res = poly_add(res, [zero] + search, -step)
            rr_new = jnp.maximum(inner(res, res, 0), zero)
            ratio = jnp.where(good, rr_new / jnp.where(good, rr, one), zero)
            search = poly_add(res, search, ratio)
            rr = rr_new
    return x


def step_kernel(
    tiles_lon, tiles_lat, levels,
    tracer_in, surface_in, flow_e_in, flow_n_in, mix_in, mask_in, cond_e_in, cond_n_in, diag_in,
    load_in, forcing_in, cmap_in, cwt_in,
    grad_out, surf_out, ctrl_out,
    tracer, surface, flow_e, flow_n, mix, mask, load, forcing, cmap, cwt, ins,
    red, ratio, quad, q_e, q_w, q_n, q_s, q_c,
    pk, send_n, send_s, recv_e, recv_w, recv_n, recv_s,
    mom_send, mom_y, mom_x_send, mom_x,
    edge_s, edge_n, edge_ew, parts,
    ctl_send, ctl_x, ctl_y_send, ctl_y,
    hs, hr, ls, lr, mys, myr, mxs, mxr, cxs, cxr, cys, cyr,
):
    col = lax.axis_index("gx")
    row = lax.axis_index("gy")
    cy, cx = surface.shape
    moves = [
        pltpu.make_async_copy(src, dst, ins.at[i])
        for i, (src, dst) in enumerate((
            (forcing_in, forcing), (mask_in, mask), (tracer_in, tracer), (surface_in, surface),
            (cond_e_in, quad.at[1]), (cond_n_in, quad.at[2]), (diag_in, quad.at[3]),
            (load_in, load), (mix_in, mix), (flow_e_in, flow_e), (flow_n_in, flow_n),
            (cmap_in, cmap), (cwt_in, cwt)))
    ]
    for move in moves:
        move.start()

    has = []
    for dx, dy in DIRS:
        ok = None
        for d, pos, size in ((dx, col, tiles_lon), (dy, row, tiles_lat)):
            if d:
                here = (pos < size - 1) if d > 0 else (pos > 0)
                ok = here if ok is None else ok & here
        has.append(ok)

    barrier = pltpu.get_barrier_semaphore()
    for d in range(1, tiles_lon):
        pl.semaphore_signal(barrier, inc=1, device_id=(lax.rem(col + d, tiles_lon), row), device_id_type=MESH)
    for d in range(1, tiles_lat):
        pl.semaphore_signal(barrier, inc=1, device_id=(col, lax.rem(row + d, tiles_lat)), device_id_type=MESH)
    for i in range(4, 8):
        dx, dy = DIRS[i]

        @pl.when(has[i])
        def _():
            pl.semaphore_signal(barrier, inc=1, device_id=(col + dx, row + dy), device_id_type=MESH)

    q_slots = [q_e, q_w, q_n, q_s] + [q_c.at[i] for i in range(4)]
    for i, slot in enumerate(q_slots):

        @pl.when(jnp.logical_not(has[i]))
        def _():
            slot[...] = jnp.zeros(slot.shape, F32)

    l_slots = [recv_e, recv_w, recv_n, recv_s]
    for i, slot in enumerate(l_slots):

        @pl.when(jnp.logical_not(has[i]))
        def _():
            slot[...] = jnp.zeros(slot.shape, F32)

    for buf in (pk, send_n, send_s, edge_s, edge_n, edge_ew):
        buf[...] = jnp.zeros(buf.shape, F32)

    for move in moves[:4]:
        move.wait()

    lane = lax.broadcasted_iota(jnp.int32, (cy, cx), 1)

    def forcing_level(k, acc):
        wet = mask[k].astype(F32)
        return acc + wet * (forcing[0, k] * tracer[0, k] + forcing[1, k] * tracer[1, k])

    quad[0] = unrolled(levels, forcing_level, surface[...])
    for move in moves[4:7]:
        move.wait()

    n_signals = tiles_lon - 1 + tiles_lat - 1
    total = jnp.int32(n_signals)
    for i in range(4, 8):
        total = total + has[i].astype(jnp.int32)
    pl.semaphore_wait(barrier, total)

    q_src = [
        quad, quad, quad.at[:, cy - 8 : cy, :], quad.at[:, 0:8, :],
        quad.at[:, cy - 8 : cy, :], quad.at[:, cy - 8 : cy, :],
        quad.at[:, 0:8, :], quad.at[:, 0:8, :],
    ]

    def q_copy(i):
        dx, dy = DIRS[i]
        o = OPPOSITE[i]
        return pltpu.make_async_remote_copy(
            src_ref=q_src[i], dst_ref=q_slots[o], send_sem=hs.at[i], recv_sem=hr.at[o],
            device_id=(col + dx, row + dy), device_id_type=MESH)

    def q_arrival(i):
        dx, dy = DIRS[i]
        return pltpu.make_async_remote_copy(
            src_ref=q_slots[i], dst_ref=q_slots[i], send_sem=hs.at[i], recv_sem=hr.at[i],
            device_id=(col + dx, row + dy), device_id_type=MESH)

    for i in range(8):

        @pl.when(has[i])
        def _():
            q_copy(i).start()

    def forward(k, kap, carry):
        kap_prev, ratio_prev, r0, r1, r2, r3 = carry
        wet = mask[k].astype(F32)
        inv = 1.0 / (1.0 + kap + kap_prev * (1.0 - ratio_prev))
        new_ratio = kap * inv
        r0 = (tracer[0, k] + kap_prev * r0) * inv
        r1 = (tracer[1, k] + kap_prev * r1) * inv
        r2 = (wet * load[0, k] + kap_prev * r2) * inv
        r3 = (wet * load[1, k] + kap_prev * r3) * inv
        ratio[k] = new_ratio
        red[0, k] = r0
        red[1, k] = r1
        red[2, k] = r2
        red[3, k] = r3
        pk[4] = jnp.where(pair == k, column_roll(flow_e[k], 2 * k + 1), pk[4])
        send_n[2, pl.ds(k, 1), :] = flow_n[k, cy - 1 : cy, :]
        return kap, new_ratio, r0, r1, r2, r3

    def forward_level(k, carry):
        return forward(k, mix[k] * mask[k + 1].astype(F32), carry)

    for move in moves[7:11]:
        move.wait()
    pair = lane // 2
    zero = jnp.zeros((cy, cx), F32)
    carry = unrolled(levels - 1, forward_level, (zero,) * 6)
    forward(levels - 1, zero, carry)

    for i in range(8):

        @pl.when(has[i])
        def _():
            q_arrival(i).wait_recv()

    lane8 = lax.broadcasted_iota(jnp.int32, (8, cx), 1) < cx // 2
    sub8 = lax.broadcasted_iota(jnp.int32, (8, cx), 0) < 4
    lane_half = lane < cx // 2

    def extend(f):
        side = jnp.where(lane_half, q_e[f], q_w[f])
        ends = jnp.where(sub8, q_n[f], q_s[f])
        corner = jnp.where(
            sub8, jnp.where(lane8, q_c[0, f], q_c[1, f]), jnp.where(lane8, q_c[2, f], q_c[3, f]))
        return jnp.concatenate(
            [jnp.concatenate([quad[f], ends], axis=0), jnp.concatenate([side, corner], axis=0)], axis=1)

    v0, ce, cn, dg = extend(0), extend(1), extend(2), extend(3)
    v1 = surface_apply(v0, ce, cn, dg)
    v2 = surface_apply(v1, ce, cn, dg)
    v3 = surface_apply(v2, ce, cn, dg)
    o0, o1, o2, o3 = (v[:cy, :cx] for v in (v0, v1, v2, v3))
    pairs = ((o0, o0), (o0, o1), (o1, o1), (o1, o2), (o2, o2), (o2, o3))
    mom_send[...] = jnp.concatenate(
        [jnp.sum(a * b, axis=0, keepdims=True) for a, b in pairs] + [jnp.zeros((2, cx), F32)], axis=0)

    def along_y(d, src, dst, ssem, rsem):
        return pltpu.make_async_remote_copy(
            src_ref=src, dst_ref=dst, send_sem=ssem.at[d - 1], recv_sem=rsem.at[d - 1],
            device_id=(col, lax.rem(row + d, tiles_lat)), device_id_type=MESH)

    def along_x(d, src, dst, ssem, rsem):
        return pltpu.make_async_remote_copy(
            src_ref=src, dst_ref=dst, send_sem=ssem.at[d - 1], recv_sem=rsem.at[d - 1],
            device_id=(lax.rem(col + d, tiles_lon), row), device_id_type=MESH)

    for d in range(1, tiles_lat):
        along_y(d, mom_send, mom_y.at[d - 1], mys, myr).start()

    def backward_level(first, step, carry):
        k = levels - 1 - first - step
        c = list(carry)
        wet = mask[k].astype(F32)
        rat = ratio[k]
        for f in range(4):
            c[f] = red[f, k] + rat * c[f]
            lam = wet * c[f]
            red[f, k] = lam
            kind, s = f // 2, f % 2
            idx = s * levels + k
            pk[f] = jnp.where(pair == k, column_roll(lam, 2 * k + 1), pk[f])
            send_s[kind, pl.ds(idx, 1), :] = lam[0:1]
            send_n[kind, pl.ds(idx, 1), :] = lam[cy - 1 : cy]
        return tuple(c)

    early = levels // 2
    lower = unrolled(early, functools.partial(backward_level, 0), (zero,) * 4)
    part = mom_send[...]
    for d in range(1, tiles_lat):
        along_y(d, mom_send, mom_y.at[d - 1], mys, myr).wait_recv()
    for d in range(1, tiles_lat):
        part = part + mom_y[d - 1]
    mom_x_send[...] = part
    for d in range(1, tiles_lon):
        along_x(d, mom_x_send, mom_x.at[d - 1], mxs, mxr).start()
    unrolled(levels - early, functools.partial(backward_level, early), lower)

    l_src = [pk, pk.at[0:4], send_n, send_s]

    def l_copy(i):
        dx, dy = DIRS[i]
        o = OPPOSITE[i]
        return pltpu.make_async_remote_copy(
            src_ref=l_src[i], dst_ref=l_slots[o], send_sem=ls.at[i], recv_sem=lr.at[o],
            device_id=(col + dx, row + dy), device_id_type=MESH)

    def l_arrival(i):
        dx, dy = DIRS[i]
        return pltpu.make_async_remote_copy(
            src_ref=l_slots[i], dst_ref=l_slots[i], send_sem=ls.at[i], recv_sem=lr.at[i],
            device_id=(col + dx, row + dy), device_id_type=MESH)

    for i in range(4):

        @pl.when(has[i])
        def _():
            l_copy(i).start()

    for d in range(1, tiles_lon):
        along_x(d, mom_x_send, mom_x.at[d - 1], mxs, mxr).wait_recv()
    for d in range(1, tiles_lon):
        part = part + mom_x[d - 1]
    sums = jnp.sum(part, axis=1, keepdims=True)
    w0, w1, w2 = gradient_weights([sums[i : i + 1] for i in range(6)])
    x = w0 * v0 + w1 * v1 + w2 * v2
    x_own = x[:cy, :cx]
    surf_out[...] = x_own

    for i in range(4):

        @pl.when(has[i])
        def _():
            l_arrival(i).wait_recv()

    even = lane == 2 * pair
    x_e, x_w = x[:cy, cx : cx + 1], x[:cy, 2 * cx - 1 : 2 * cx]
    for s in range(2):
        recv_e[s] = jnp.where(
            even,
            column_roll(recv_e[s] + x_e * recv_e[2 + s], cx - 1),
            column_roll(recv_w[s] + x_w * recv_w[2 + s], 1))
    recv_n[0] = recv_n[0] + x[cy : cy + 1, :cx] * recv_n[1]
    recv_s[0] = recv_s[0] + x[cy + 7 : cy + 8, :cx] * recv_s[1]

    sub = lax.broadcasted_iota(jnp.int32, (cy, cx), 0)
    first_lane, last_lane = lane == 0, lane == cx - 1
    first_row, last_row = sub == 0, sub == cy - 1

    def final_level(k, carry):
        half_e = 0.5 * flow_e[k]
        half_n = 0.5 * flow_n[k]
        half_w_halo = 0.5 * column_roll(recv_w[4], lax.rem(cx - 2 * k, cx))
        half_s_halo = 0.5 * recv_s[2, pl.ds(k, 1), :]
        for s in range(2):
            idx = s * levels + k
            lam = red[s, k] + x_own * red[2 + s, k]
            side = column_roll(recv_e[s], cx - 1 - 2 * k)
            lam_e = jnp.where(last_lane, side, column_roll(lam, cx - 1))
            lam_n = jnp.where(last_row, recv_n[0, pl.ds(idx, 1), :], pltpu.roll(lam, cy - 1, 0))
            flux_e = half_e * (lam_e - lam)
            flux_n = half_n * (lam_n - lam)
            halo_w = half_w_halo * (lam - side)
            halo_s = half_s_halo * (lam[0:1] - recv_s[0, pl.ds(idx, 1), :])
            flux_w = jnp.where(first_lane, halo_w, column_roll(flux_e, 1))
            flux_s = jnp.where(first_row, halo_s, pltpu.roll(flux_n, 1, 0))
            g = lam + flux_e + flux_w + flux_n + flux_s
            grad_out[s, k] = g
            edge_ew[s] = jnp.where(pair == k, column_roll(g, 2 * k + 1), edge_ew[s])
            edge_s[pl.ds(2 * k + 1 - s, 1), :] = g[0:1]
            edge_n[pl.ds(2 * k + 1 - s, 1), :] = g[cy - 1 : cy]
        return carry

    unrolled(levels, final_level, 0)
    for move in moves[11:]:
        move.wait()

    lon, lat = tiles_lon * cx, tiles_lat * cy
    controls = ctl_send.shape[0]
    lane_row = lax.broadcasted_iota(jnp.int32, (1, LANES), 1)
    last_chunk = cmap.shape[0] - 1

    def points(ref, begin):
        chunk = begin // LANES
        off = lax.rem(begin, LANES)
        near = ref[pl.ds(chunk, 1), :]
        far = ref[pl.ds(jnp.minimum(chunk + 1, last_chunk), 1), :]
        back = lax.rem(LANES - off, LANES)
        return jnp.where(
            lane_row < LANES - off, pltpu.roll(near, back, 1), pltpu.roll(far, back, 1))

    diagonal = lax.broadcasted_iota(jnp.int32, (cy, LANES), 0) == lax.broadcasted_iota(
        jnp.int32, (cy, LANES), 1)
    sides = (
        (col * cx, row == 0),
        (lon + col * cx, row == tiles_lat - 1),
        (2 * lon + row * cy, col == 0),
        (2 * lon + lat + row * cy, col == tiles_lon - 1),
    )
    for i, (begin, active) in enumerate(sides):

        @pl.when(active)
        def _():
            wts = points(cwt, begin)
            if i < 2:
                values = ((edge_s, edge_n)[i][...] * wts).T
            else:
                if i == 2:
                    values = jnp.where(even, column_roll(edge_ew[1], LANES - 1), edge_ew[0])
                else:
                    values = jnp.where(even, edge_ew[1], column_roll(edge_ew[0], 1))
                weight = jnp.sum(jnp.where(diagonal, wts, 0.0), axis=1, keepdims=True)
                values = jnp.concatenate(
                    [values * weight, jnp.zeros((LANES - cy, LANES), F32)], axis=0)
            high = values.astype(jnp.bfloat16)
            rest = values - high.astype(F32)
            middle = rest.astype(jnp.bfloat16)
            low = (rest - middle.astype(F32)).astype(jnp.bfloat16)
            parts[i] = jnp.concatenate([high, middle, low], axis=1)

    share = controls // tiles_lon
    share_ids = lax.broadcasted_iota(jnp.int32, (share, LANES), 0)

    def has_points(c):
        return (row == 0) | (row == tiles_lat - 1) | (c == 0) | (c == tiles_lon - 1)

    def control_block(target):
        start = pl.multiple_of(target * share, 8)
        block = ctl_send.at[pl.ds(start, share), :]
        block[...] = jnp.zeros((share, LANES), F32)
        for i, (begin, active) in enumerate(sides):

            @pl.when(active)
            def _():
                hit = share_ids + start == points(cmap, begin)
                sums = lax.dot_general(
                    jnp.where(hit, 1.0, 0.0).astype(jnp.bfloat16), parts[i],
                    (((1,), (0,)), ((), ())), preferred_element_type=F32)
                block[...] += (
                    sums[:, 2 * LANES :] + sums[:, LANES : 2 * LANES]) + sums[:, :LANES]

        return block

    for d in range(1, tiles_lon):
        block = control_block(lax.rem(col + d, tiles_lon))

        @pl.when(has_points(col))
        def _():
            along_x(d, block, ctl_x.at[d - 1], cxs, cxr).start()

    mine = control_block(col)[...]
    for d in range(1, tiles_lon):
        sender = has_points(lax.rem(col + tiles_lon - d, tiles_lon))

        @pl.when(sender)
        def _():
            along_x(d, ctl_send.at[pl.ds(0, share), :], ctl_x.at[d - 1], cxs, cxr).wait_recv()

        @pl.when(jnp.logical_not(sender))
        def _():
            ctl_x[d - 1] = jnp.zeros((share, LANES), F32)

    for d in range(1, tiles_lon):
        mine = mine + ctl_x[d - 1]
    ctl_y_send[...] = jnp.zeros(ctl_y_send.shape, F32)
    for j in range(tiles_lat):
        ctl_y_send[j, 0:CTRL_DEV] = mine[j * CTRL_DEV : (j + 1) * CTRL_DEV]
    for d in range(1, tiles_lat):
        along_y(d, ctl_y_send.at[lax.rem(row + d, tiles_lat)], ctl_y.at[d - 1], cys, cyr).start()
    result = ctl_y_send[row]
    for d in range(1, tiles_lat):
        along_y(d, ctl_y_send.at[0], ctl_y.at[d - 1], cys, cyr).wait_recv()
    for d in range(1, tiles_lat):
        result = result + ctl_y[d - 1]
    source = lax.broadcasted_iota(jnp.int32, (LANES, LANES), 0)
    target = lax.broadcasted_iota(jnp.int32, (LANES, LANES), 1)
    order = jnp.where(target < levels, 2 * target + 1, 2 * (target - levels))
    result = lax.dot_general(
        result, jnp.where(source == order, 1.0, 0.0), (((1,), (0,)), ((), ())),
        precision=HIGHEST, preferred_element_type=F32)
    for s in range(2):
        ctrl_out[:, s, :] = result[0:CTRL_DEV, s * levels : (s + 1) * levels]

    for i in range(8):

        @pl.when(has[i])
        def _():
            q_copy(i).wait_send()

    for i in range(4):

        @pl.when(has[i])
        def _():
            l_copy(i).wait_send()

    for d in range(1, tiles_lat):
        along_y(d, mom_send, mom_y.at[d - 1], mys, myr).wait_send()
        along_y(d, ctl_y_send.at[0], ctl_y.at[d - 1], cys, cyr).wait_send()
    for d in range(1, tiles_lon):
        along_x(d, mom_x_send, mom_x.at[d - 1], mxs, mxr).wait_send()

        @pl.when(has_points(col))
        def _():
            along_x(d, ctl_send.at[pl.ds(0, share), :], ctl_x.at[d - 1], cxs, cxr).wait_send()


def results_kernel(grad, surf, ctrl, grad_out, surf_out, ctrl_out, sems):
    half = grad.shape[1] // 2
    pairs = [(surf, surf_out), (ctrl, ctrl_out)]
    for s in range(2):
        for part in (slice(0, half), slice(half, grad.shape[1])):
            pairs.append((grad.at[s, part], grad_out.at[s, part]))
    moves = [pltpu.make_async_copy(src, dst, sems.at[i]) for i, (src, dst) in enumerate(pairs)]
    for move in moves:
        move.start()
    for move in moves:
        move.wait()


def per_device(
    tracer_adjoint, surface_adjoint, flow_east, flow_north, vertical_mix, land_mask,
    conduct_east, conduct_north, surface_diagonal, pressure_load, surface_forcing,
    control_map, control_weight,
):
    tiles_lon, tiles_lat = lax.axis_size("gx"), lax.axis_size("gy")
    _, levels, cy, cx = tracer_adjoint.shape
    pack = -(-2 * levels // 8) * 8
    controls = CTRL_DEV * tiles_lon * tiles_lat
    points = control_map.shape[0]
    vmem = pl.BlockSpec(memory_space=pltpu.VMEM)
    hbm = pl.BlockSpec(memory_space=pltpu.HBM)
    dma = pltpu.SemaphoreType.DMA
    buf = lambda *shape: pltpu.VMEM(shape, F32)
    scratch = [
        buf(2, levels, cy, cx), buf(cy, cx), buf(levels, cy, cx), buf(levels, cy, cx),
        buf(levels - 1, cy, cx), pltpu.VMEM((levels, cy, cx), jnp.int32),
        pltpu.SMEM((2, levels), F32), pltpu.SMEM((2, levels), F32),
        pltpu.VMEM((points // LANES, LANES), jnp.int32), buf(points // LANES, LANES), dma((13,)),
        buf(4, levels, cy, cx), buf(levels, cy, cx), buf(4, cy, cx),
        buf(4, cy, cx), buf(4, cy, cx), buf(4, 8, cx), buf(4, 8, cx), buf(4, 4, 8, cx),
        buf(5, cy, cx), buf(3, pack, cx), buf(2, pack, cx),
        buf(4, cy, cx), buf(5, cy, cx), buf(2, pack, cx), buf(3, pack, cx),
        buf(8, cx), buf(tiles_lat - 1, 8, cx), buf(8, cx), buf(tiles_lon - 1, 8, cx),
        buf(LANES, cx), buf(LANES, cx), buf(2, cy, cx),
        pltpu.VMEM((4, LANES, 3 * LANES), jnp.bfloat16),
        buf(controls, LANES), buf(tiles_lon - 1, controls // tiles_lon, LANES),
        buf(tiles_lat, SLOT, LANES), buf(tiles_lat - 1, SLOT, LANES),
        dma((8,)), dma((8,)), dma((4,)), dma((4,)),
        dma((tiles_lat - 1,)), dma((tiles_lat - 1,)), dma((tiles_lon - 1,)), dma((tiles_lon - 1,)),
        dma((tiles_lon - 1,)), dma((tiles_lon - 1,)), dma((tiles_lat - 1,)), dma((tiles_lat - 1,)),
    ]
    grad, surf, ctrl = pl.pallas_call(
        functools.partial(step_kernel, tiles_lon, tiles_lat, levels),
        out_shape=(
            pltpu.VMEM(tracer_adjoint.shape, F32),
            pltpu.VMEM(surface_adjoint.shape, F32),
            pltpu.VMEM((CTRL_DEV, 2, levels), F32),
        ),
        in_specs=[hbm] * 13,
        out_specs=(vmem, vmem, vmem),
        scratch_shapes=scratch,
        compiler_params=pltpu.CompilerParams(
            collective_id=0, has_side_effects=True, vmem_limit_bytes=VMEM_LIMIT),
    )(
        tracer_adjoint, surface_adjoint, flow_east, flow_north, vertical_mix, land_mask,
        conduct_east, conduct_north, surface_diagonal, pressure_load, surface_forcing,
        control_map.reshape(-1, LANES), control_weight.reshape(-1, LANES),
    )
    grad, surf, ctrl = pl.pallas_call(
        results_kernel,
        out_shape=tuple(jax.ShapeDtypeStruct(a.shape, F32) for a in (grad, surf, ctrl)),
        in_specs=[pl.BlockSpec(memory_space=pl.ANY)] * 3,
        out_specs=(hbm, hbm, hbm),
        scratch_shapes=[dma((6,))],
        compiler_params=pltpu.CompilerParams(vmem_limit_bytes=1024 * 1024),
    )(grad, surf, ctrl)
    return grad, surf, ctrl.transpose(1, 2, 0)


def solution(mesh):
    in_specs = (
        P(None, None, "gy", "gx"), P("gy", "gx"),
        P(None, "gy", "gx"), P(None, "gy", "gx"), P(None, "gy", "gx"), P(None, "gy", "gx"),
        P("gy", "gx"), P("gy", "gx"), P("gy", "gx"), P(), P(), P(), P(),
    )
    out_specs = (P(None, None, "gy", "gx"), P("gy", "gx"), P(None, None, ("gx", "gy")))
    return jax.shard_map(
        per_device, mesh=mesh, in_specs=in_specs, out_specs=out_specs, check_vma=False
    )
```

```python
import functools
import jax
import jax.numpy as jnp
from jax import lax
from jax.experimental import pallas as pl
from jax.experimental.pallas import tpu as pltpu
from jax.sharding import PartitionSpec as P

ITERS = 3
CTRL_DEV = 10
SLOT = 16
VMEM_LIMIT = 63_200 * 1024
LANES = 128
MESH = pl.DeviceIdType.MESH
DIRS = ((1, 0), (-1, 0), (0, 1), (0, -1), (1, 1), (-1, 1), (1, -1), (-1, -1))
OPPOSITE = (1, 0, 3, 2, 7, 6, 5, 4)
F32 = jnp.float32
HIGHEST = lax.Precision.HIGHEST


def unrolled(count, body, carry):
    width = max(u for u in range(1, 8) if count % u == 0)

    def several(i, carry):
        for u in range(width):
            carry = body(i * width + u, carry)
        return carry

    return lax.fori_loop(0, count // width, several, carry)


def column_roll(value, shift):
    return pltpu.roll(value, shift, 1)


def surface_apply(e, ce, cn, dg):
    rows, cols = e.shape
    flux_e = ce * (e - pltpu.roll(e, cols - 1, 1))
    flux_n = cn * (e - pltpu.roll(e, rows - 1, 0))
    return dg * e + (flux_e - pltpu.roll(flux_e, 1, 1)) + (flux_n - pltpu.roll(flux_n, 1, 0))


def poly_add(p, q, factor):
    size = max(len(p), len(q))
    out = []
    for i in range(size):
        term = factor * q[i] if i < len(q) else None
        if i < len(p):
            term = p[i] if term is None else p[i] + term
        out.append(term)
    return out


def gradient_weights(mu):
    def inner(p, q, shift):
        total = None
        for i, pi in enumerate(p):
            for j, qj in enumerate(q):
                term = pi * qj * mu[i + j + shift]
                total = term if total is None else total + term
        return total

    one = jnp.ones_like(mu[0])
    zero = jnp.zeros_like(mu[0])
    floor = 2e-7 * mu[0]
    res, search, x = [one], [one], [zero]
    rr = mu[0]
    for it in range(ITERS):
        den = inner(search, search, 1)
        good = (den > 0) & (rr > floor)
        step = jnp.where(good, rr / jnp.where(good, den, one), zero)
        x = poly_add(x, search, step)
        if it + 1 < ITERS:
            res = poly_add(res, [zero] + search, -step)
            rr_new = jnp.maximum(inner(res, res, 0), zero)
            ratio = jnp.where(good, rr_new / jnp.where(good, rr, one), zero)
            search = poly_add(res, search, ratio)
            rr = rr_new
    return x


def step_kernel(
    tiles_lon, tiles_lat, levels,
    tracer_in, surface_in, flow_e_in, flow_n_in, mix_in, mask_in, cond_e_in, cond_n_in, diag_in,
    load_in, forcing_in, cmap_in, cwt_in,
    grad_out, surf_out, ctrl_out,
    tracer, surface, flow_e, flow_n, mix, mask, load, forcing, cmap, cwt, ins,
    red, ratio, quad, q_e, q_w, q_n, q_s, q_c,
    pk, send_n, send_s, recv_e, recv_w, recv_n, recv_s,
    mom_send, mom_y, mom_x_send, mom_x,
    pr, rr, parts, hot,
    ctl_send, ctl_x, ctl_y_send, ctl_y,
    hs, hr, ls, lr, mys, myr, mxs, mxr, cxs, cxr, cys, cyr,
):
    col = lax.axis_index("gx")
    row = lax.axis_index("gy")
    cy, cx = surface.shape
    moves = [
        pltpu.make_async_copy(src, dst, ins.at[i])
        for i, (src, dst) in enumerate((
            (forcing_in, forcing), (mask_in, mask), (tracer_in, tracer), (surface_in, surface),
            (cond_e_in, quad.at[1]), (cond_n_in, quad.at[2]), (diag_in, quad.at[3]),
            (load_in, load), (mix_in, mix), (flow_e_in, flow_e), (flow_n_in, flow_n),
            (cmap_in, cmap), (cwt_in, cwt)))
    ]
    for move in moves:
        move.start()

    has = []
    for dx, dy in DIRS:
        ok = None
        for d, pos, size in ((dx, col, tiles_lon), (dy, row, tiles_lat)):
            if d:
                here = (pos < size - 1) if d > 0 else (pos > 0)
                ok = here if ok is None else ok & here
        has.append(ok)

    barrier = pltpu.get_barrier_semaphore()
    for d in range(1, tiles_lon):
        pl.semaphore_signal(barrier, inc=1, device_id=(lax.rem(col + d, tiles_lon), row), device_id_type=MESH)
    for d in range(1, tiles_lat):
        pl.semaphore_signal(barrier, inc=1, device_id=(col, lax.rem(row + d, tiles_lat)), device_id_type=MESH)
    for i in range(4, 8):
        dx, dy = DIRS[i]

        @pl.when(has[i])
        def _():
            pl.semaphore_signal(barrier, inc=1, device_id=(col + dx, row + dy), device_id_type=MESH)

    q_slots = [q_e, q_w, q_n, q_s] + [q_c.at[i] for i in range(4)]
    for i, slot in enumerate(q_slots):

        @pl.when(jnp.logical_not(has[i]))
        def _():
            slot[...] = jnp.zeros(slot.shape, F32)

    l_slots = [recv_e, recv_w, recv_n, recv_s]
    for i, slot in enumerate(l_slots):

        @pl.when(jnp.logical_not(has[i]))
        def _():
            slot[...] = jnp.zeros(slot.shape, F32)

    for buf in (pk, send_n, send_s, pr, rr):
        buf[...] = jnp.zeros(buf.shape, F32)

    for move in moves[:4]:
        move.wait()

    lane = lax.broadcasted_iota(jnp.int32, (cy, cx), 1)

    def forcing_level(k, acc):
        wet = mask[k].astype(F32)
        return acc + wet * (forcing[0, k] * tracer[0, k] + forcing[1, k] * tracer[1, k])

    quad[0] = unrolled(levels, forcing_level, surface[...])
    for move in moves[4:7]:
        move.wait()

    n_signals = tiles_lon - 1 + tiles_lat - 1
    total = jnp.int32(n_signals)
    for i in range(4, 8):
        total = total + has[i].astype(jnp.int32)
    pl.semaphore_wait(barrier, total)

    q_src = [
        quad, quad, quad.at[:, cy - 8 : cy, :], quad.at[:, 0:8, :],
        quad.at[:, cy - 8 : cy, :], quad.at[:, cy - 8 : cy, :],
        quad.at[:, 0:8, :], quad.at[:, 0:8, :],
    ]

    def q_copy(i):
        dx, dy = DIRS[i]
        o = OPPOSITE[i]
        return pltpu.make_async_remote_copy(
            src_ref=q_src[i], dst_ref=q_slots[o], send_sem=hs.at[i], recv_sem=hr.at[o],
            device_id=(col + dx, row + dy), device_id_type=MESH)

    def q_arrival(i):
        dx, dy = DIRS[i]
        return pltpu.make_async_remote_copy(
            src_ref=q_slots[i], dst_ref=q_slots[i], send_sem=hs.at[i], recv_sem=hr.at[i],
            device_id=(col + dx, row + dy), device_id_type=MESH)

    for i in range(8):

        @pl.when(has[i])
        def _():
            q_copy(i).start()

    west, south = col == 0, row == 0
    east_side = jnp.where(west, 0, 1)
    lon, lat = tiles_lon * cx, tiles_lat * cy
    controls = ctl_send.shape[0]
    lane_row = lax.broadcasted_iota(jnp.int32, (1, LANES), 1)
    last_chunk = cmap.shape[0] - 1

    def points(ref, begin):
        chunk = begin // LANES
        off = lax.rem(begin, LANES)
        near = ref[pl.ds(chunk, 1), :]
        far = ref[pl.ds(jnp.minimum(chunk + 1, last_chunk), 1), :]
        back = lax.rem(LANES - off, LANES)
        return jnp.where(
            lane_row < LANES - off, pltpu.roll(near, back, 1), pltpu.roll(far, back, 1))

    for move in moves[11:]:
        move.wait()
    begin_row = col * cx + jnp.where(south, 0, lon)
    begin_col = 2 * lon + row * cy + jnp.where(west, 0, lat)
    row_on = jnp.where(south | (row == tiles_lat - 1), 1.0, 0.0)
    col_on = jnp.where(west | (col == tiles_lon - 1), 1.0, 0.0)
    control_ids = lax.broadcasted_iota(jnp.int32, (controls, LANES), 0)
    for i, begin in enumerate((begin_row, begin_col)):
        hit = jnp.where(control_ids == points(cmap, begin), 1.0, 0.0)
        hot[:, i * LANES : (i + 1) * LANES] = hit.astype(jnp.bfloat16)
    row_wts = points(cwt, begin_row) * row_on
    diagonal = lax.broadcasted_iota(jnp.int32, (cy, LANES), 0) == lax.broadcasted_iota(
        jnp.int32, (cy, LANES), 1)
    col_wts = jnp.sum(
        jnp.where(diagonal, points(cwt, begin_col) * col_on, 0.0), axis=1, keepdims=True)

    def forward(k, kap, carry):
        kap_prev, ratio_prev, r0, r1, r2, r3 = carry
        wet = mask[k].astype(F32)
        inv = 1.0 / (1.0 + kap + kap_prev * (1.0 - ratio_prev))
        new_ratio = kap * inv
        r0 = (tracer[0, k] + kap_prev * r0) * inv
        r1 = (tracer[1, k] + kap_prev * r1) * inv
        r2 = (wet * load[0, k] + kap_prev * r2) * inv
        r3 = (wet * load[1, k] + kap_prev * r3) * inv
        ratio[k] = new_ratio
        red[0, k] = r0
        red[1, k] = r1
        red[2, k] = r2
        red[3, k] = r3
        pk[4] = jnp.where(pair == k, column_roll(flow_e[k], 2 * k + 1), pk[4])
        pr[4] = jnp.where(pair == k, column_roll(flow_e[k], 2 * k + 1 + 2 * east_side), pr[4])
        pr[5] = jnp.where(pair == k, column_roll(flow_n[k], 2 * k + 1 + east_side), pr[5])
        send_n[2, pl.ds(2 * k + 1, 1), :] = flow_n[k, cy - 1 : cy, :]
        face_e = jnp.where(south, flow_e[k, 0:1, :], flow_e[k, cy - 1 : cy, :])
        face_n = jnp.where(south, flow_n[k, 0:1, :], flow_n[k, cy - 2 : cy - 1, :])
        for s in range(2):
            rr[2, pl.ds(2 * k + 1 - s, 1), :] = face_e
            rr[3, pl.ds(2 * k + 1 - s, 1), :] = face_n
        return kap, new_ratio, r0, r1, r2, r3

    def forward_level(k, carry):
        return forward(k, mix[k] * mask[k + 1].astype(F32), carry)

    for move in moves[7:11]:
        move.wait()
    pair = lane // 2
    zero = jnp.zeros((cy, cx), F32)
    carry = unrolled(levels - 1, forward_level, (zero,) * 6)
    forward(levels - 1, zero, carry)

    for i in range(8):

        @pl.when(has[i])
        def _():
            q_arrival(i).wait_recv()

    lane8 = lax.broadcasted_iota(jnp.int32, (8, cx), 1) < cx // 2
    sub8 = lax.broadcasted_iota(jnp.int32, (8, cx), 0) < 4
    lane_half = lane < cx // 2

    def extend(f):
        side = jnp.where(lane_half, q_e[f], q_w[f])
        ends = jnp.where(sub8, q_n[f], q_s[f])
        corner = jnp.where(
            sub8, jnp.where(lane8, q_c[0, f], q_c[1, f]), jnp.where(lane8, q_c[2, f], q_c[3, f]))
        return jnp.concatenate(
            [jnp.concatenate([quad[f], ends], axis=0), jnp.concatenate([side, corner], axis=0)], axis=1)

    v0, ce, cn, dg = extend(0), extend(1), extend(2), extend(3)
    v1 = surface_apply(v0, ce, cn, dg)
    v2 = surface_apply(v1, ce, cn, dg)
    v3 = surface_apply(v2, ce, cn, dg)
    o0, o1, o2, o3 = (v[:cy, :cx] for v in (v0, v1, v2, v3))
    pairs = ((o0, o0), (o0, o1), (o1, o1), (o1, o2), (o2, o2), (o2, o3))
    mom_send[...] = jnp.concatenate(
        [jnp.sum(a * b, axis=0, keepdims=True) for a, b in pairs] + [jnp.zeros((2, cx), F32)], axis=0)

    def along_y(d, src, dst, ssem, rsem):
        return pltpu.make_async_remote_copy(
            src_ref=src, dst_ref=dst, send_sem=ssem.at[d - 1], recv_sem=rsem.at[d - 1],
            device_id=(col, lax.rem(row + d, tiles_lat)), device_id_type=MESH)

    def along_x(d, src, dst, ssem, rsem):
        return pltpu.make_async_remote_copy(
            src_ref=src, dst_ref=dst, send_sem=ssem.at[d - 1], recv_sem=rsem.at[d - 1],
            device_id=(lax.rem(col + d, tiles_lon), row), device_id_type=MESH)

    for d in range(1, tiles_lat):
        along_y(d, mom_send, mom_y.at[d - 1], mys, myr).start()

    def backward_level(first, step, carry):
        k = levels - 1 - first - step
        c = list(carry)
        wet = mask[k].astype(F32)
        rat = ratio[k]
        for f in range(4):
            c[f] = red[f, k] + rat * c[f]
            lam = wet * c[f]
            red[f, k] = lam
            kind, s = f // 2, f % 2
            idx = 2 * k + 1 - s
            pr[f] = jnp.where(pair == k, column_roll(lam, 2 * k + 3 * east_side), pr[f])
            pk[f] = jnp.where(pair == k, column_roll(lam, 2 * k + 1), pk[f])
            send_s[kind, pl.ds(idx, 1), :] = lam[0:1]
            send_n[kind, pl.ds(idx, 1), :] = lam[cy - 1 : cy]
            rr[kind, pl.ds(idx, 1), :] = jnp.where(south, lam[1:2], lam[cy - 2 : cy - 1])
        return tuple(c)

    early = levels // 2
    lower = unrolled(early, functools.partial(backward_level, 0), (zero,) * 4)
    part = mom_send[...]
    for d in range(1, tiles_lat):
        along_y(d, mom_send, mom_y.at[d - 1], mys, myr).wait_recv()
    for d in range(1, tiles_lat):
        part = part + mom_y[d - 1]
    mom_x_send[...] = part
    for d in range(1, tiles_lon):
        along_x(d, mom_x_send, mom_x.at[d - 1], mxs, mxr).start()
    unrolled(levels - early, functools.partial(backward_level, early), lower)

    l_src = [pk, pk.at[0:4], send_n, send_s]

    def l_copy(i):
        dx, dy = DIRS[i]
        o = OPPOSITE[i]
        return pltpu.make_async_remote_copy(
            src_ref=l_src[i], dst_ref=l_slots[o], send_sem=ls.at[i], recv_sem=lr.at[o],
            device_id=(col + dx, row + dy), device_id_type=MESH)

    def l_arrival(i):
        dx, dy = DIRS[i]
        return pltpu.make_async_remote_copy(
            src_ref=l_slots[i], dst_ref=l_slots[i], send_sem=ls.at[i], recv_sem=lr.at[i],
            device_id=(col + dx, row + dy), device_id_type=MESH)

    for i in range(4):

        @pl.when(has[i])
        def _():
            l_copy(i).start()

    for d in range(1, tiles_lon):
        along_x(d, mom_x_send, mom_x.at[d - 1], mxs, mxr).wait_recv()
    for d in range(1, tiles_lon):
        part = part + mom_x[d - 1]
    sums = jnp.sum(part, axis=1, keepdims=True)
    w0, w1, w2 = gradient_weights([sums[i : i + 1] for i in range(6)])
    x = w0 * v0 + w1 * v1 + w2 * v2
    x_own = x[:cy, :cx]
    surf_out[...] = x_own

    for i in range(4):

        @pl.when(has[i])
        def _():
            l_arrival(i).wait_recv()

    even = lane == 2 * pair
    x_e, x_w = x[:cy, cx : cx + 1], x[:cy, 2 * cx - 1 : 2 * cx]
    for s in range(2):
        recv_e[s] = jnp.where(
            even,
            column_roll(recv_e[s] + x_e * recv_e[2 + s], cx - 1),
            column_roll(recv_w[s] + x_w * recv_w[2 + s], 1))
    recv_n[0] = recv_n[0] + x[cy : cy + 1, :cx] * recv_n[1]
    recv_s[0] = recv_s[0] + x[cy + 7 : cy + 8, :cx] * recv_s[1]

    sub = lax.broadcasted_iota(jnp.int32, (cy, cx), 0)
    first_lane, last_lane = lane == 0, lane == cx - 1
    first_row, last_row = sub == 0, sub == cy - 1

    filler = jnp.zeros((LANES - recv_n.shape[1], LANES), F32)

    def rim_lanes(rows):
        turned = jnp.concatenate([rows, filler], axis=0).T
        return jnp.where(west, turned[0:1], turned[cx - 1 : cx])

    north_row, south_row, south_face = (
        rim_lanes(recv_n[0]), rim_lanes(recv_s[0]), rim_lanes(recv_s[2]))
    x_rim = jnp.where(west, x[:cy, 0:1], x[:cy, cx - 1 : cx])
    x_in = jnp.where(west, x[:cy, 1:2], x[:cy, cx - 2 : cx - 1])
    half_sign = jnp.where(west, 0.5, -0.5)
    rim_cols = []
    for s in range(2):
        lam = pk[s] + x_rim * pk[2 + s]
        lam = jnp.where(west, lam, column_roll(lam, 1))
        inner = pr[s] + x_in * pr[2 + s]
        beyond_n = column_roll(north_row, 1) if s else north_row
        beyond_s = column_roll(south_row, 1) if s else south_row
        lam_n = jnp.where(last_row, beyond_n, pltpu.roll(lam, cy - 1, 0))
        flux_n = 0.5 * pr[5] * (lam_n - lam)
        flux_s = jnp.where(
            first_row, 0.5 * south_face * (lam - beyond_s), pltpu.roll(flux_n, 1, 0))
        rim_cols.append(lam + half_sign * pr[4] * (inner - lam) + flux_n + flux_s)
    by_col = jnp.where(even, column_roll(rim_cols[1], LANES - 1), rim_cols[0]) * col_wts
    by_col = jnp.concatenate([by_col, jnp.zeros((LANES - cy, LANES), F32)], axis=0)

    side_rows = [jnp.where(south, recv_e[s, 0:1, :], recv_e[s, cy - 1 : cy, :]) for s in range(2)]
    west_face = jnp.where(south, recv_w[4, 0:1, :], recv_w[4, cy - 1 : cy, :])
    even_row = even[0:1]
    turned = jnp.concatenate([
        jnp.where(even_row, side_rows[1], column_roll(side_rows[0], 1)),
        jnp.where(even_row, column_roll(side_rows[1], LANES - 1), side_rows[0]),
        jnp.where(even_row, west_face, column_roll(west_face, 1)),
        jnp.zeros((LANES - 3, LANES), F32)], axis=0).T[: rr.shape[1]]
    x_rim = jnp.where(south, x[0:1, :cx], x[cy - 1 : cy, :cx])
    x_in = jnp.where(south, x[1:2, :cx], x[cy - 2 : cy - 1, :cx])
    half_sign = jnp.where(south, 0.5, -0.5)
    lam = jnp.where(south, send_s[0], send_n[0]) + x_rim * jnp.where(south, send_s[1], send_n[1])
    inner = rr[0] + x_in * rr[1]
    lane_tall = lax.broadcasted_iota(jnp.int32, lam.shape, 1)
    lam_e = jnp.where(lane_tall == cx - 1, turned[:, 0:1], column_roll(lam, cx - 1))
    flux_e = 0.5 * rr[2] * (lam_e - lam)
    flux_w = jnp.where(
        lane_tall == 0, 0.5 * turned[:, 2:3] * (lam - turned[:, 1:2]), column_roll(flux_e, 1))
    by_row = (lam + half_sign * rr[3] * (inner - lam) + flux_e + flux_w) * row_wts
    by_row = jnp.concatenate([by_row, filler], axis=0).T

    for i, values in enumerate((by_row, by_col)):
        high = values.astype(jnp.bfloat16)
        rest = values - high.astype(F32)
        middle = rest.astype(jnp.bfloat16)
        low = (rest - middle.astype(F32)).astype(jnp.bfloat16)
        parts[i * LANES : (i + 1) * LANES] = jnp.concatenate([high, middle, low], axis=1)
    totals = lax.dot_general(
        hot[...], parts[...], (((1,), (0,)), ((), ())), preferred_element_type=F32)
    ctl_send[...] = (totals[:, 2 * LANES :] + totals[:, LANES : 2 * LANES]) + totals[:, :LANES]

    share = controls // tiles_lon

    def has_points(c):
        return south | (row == tiles_lat - 1) | (c == 0) | (c == tiles_lon - 1)

    for d in range(1, tiles_lon):
        begin = pl.multiple_of(lax.rem(col + d, tiles_lon) * share, 8)

        @pl.when(has_points(col))
        def _():
            along_x(d, ctl_send.at[pl.ds(begin, share), :], ctl_x.at[d - 1], cxs, cxr).start()

    def final_level(first, step, carry):
        k = first + step
        half_e = 0.5 * flow_e[k]
        half_n = 0.5 * flow_n[k]
        half_w_halo = 0.5 * column_roll(recv_w[4], lax.rem(cx - 2 * k, cx))
        half_s_halo = 0.5 * recv_s[2, pl.ds(2 * k + 1, 1), :]
        for s in range(2):
            idx = 2 * k + 1 - s
            lam = red[s, k] + x_own * red[2 + s, k]
            side = column_roll(recv_e[s], cx - 1 - 2 * k)
            lam_e = jnp.where(last_lane, side, column_roll(lam, cx - 1))
            lam_n = jnp.where(last_row, recv_n[0, pl.ds(idx, 1), :], pltpu.roll(lam, cy - 1, 0))
            flux_e = half_e * (lam_e - lam)
            flux_n = half_n * (lam_n - lam)
            halo_w = half_w_halo * (lam - side)
            halo_s = half_s_halo * (lam[0:1] - recv_s[0, pl.ds(idx, 1), :])
            flux_w = jnp.where(first_lane, halo_w, column_roll(flux_e, 1))
            flux_s = jnp.where(first_row, halo_s, pltpu.roll(flux_n, 1, 0))
            g = lam + flux_e + flux_w + flux_n + flux_s
            grad_out[s, k] = g
        return carry

    unrolled(early, functools.partial(final_level, 0), 0)
    mine = ctl_send[pl.ds(pl.multiple_of(col * share, 8), share), :]
    for d in range(1, tiles_lon):
        sender = has_points(lax.rem(col + tiles_lon - d, tiles_lon))

        @pl.when(sender)
        def _():
            along_x(d, ctl_send.at[pl.ds(0, share), :], ctl_x.at[d - 1], cxs, cxr).wait_recv()

        @pl.when(jnp.logical_not(sender))
        def _():
            ctl_x[d - 1] = jnp.zeros((share, LANES), F32)

    for d in range(1, tiles_lon):
        mine = mine + ctl_x[d - 1]
    ctl_y_send[...] = jnp.zeros(ctl_y_send.shape, F32)
    for j in range(tiles_lat):
        ctl_y_send[j, 0:CTRL_DEV] = mine[j * CTRL_DEV : (j + 1) * CTRL_DEV]
    for d in range(1, tiles_lat):
        along_y(d, ctl_y_send.at[lax.rem(row + d, tiles_lat)], ctl_y.at[d - 1], cys, cyr).start()
    unrolled(levels - early, functools.partial(final_level, early), 0)
    result = ctl_y_send[row]
    for d in range(1, tiles_lat):
        along_y(d, ctl_y_send.at[0], ctl_y.at[d - 1], cys, cyr).wait_recv()
    for d in range(1, tiles_lat):
        result = result + ctl_y[d - 1]
    source = lax.broadcasted_iota(jnp.int32, (LANES, LANES), 0)
    target = lax.broadcasted_iota(jnp.int32, (LANES, LANES), 1)
    order = jnp.where(target < levels, 2 * target + 1, 2 * (target - levels))
    result = lax.dot_general(
        result, jnp.where(source == order, 1.0, 0.0), (((1,), (0,)), ((), ())),
        precision=HIGHEST, preferred_element_type=F32)
    for s in range(2):
        ctrl_out[:, s, :] = result[0:CTRL_DEV, s * levels : (s + 1) * levels]

    for i in range(8):

        @pl.when(has[i])
        def _():
            q_copy(i).wait_send()

    for i in range(4):

        @pl.when(has[i])
        def _():
            l_copy(i).wait_send()

    for d in range(1, tiles_lat):
        along_y(d, mom_send, mom_y.at[d - 1], mys, myr).wait_send()
        along_y(d, ctl_y_send.at[0], ctl_y.at[d - 1], cys, cyr).wait_send()
    for d in range(1, tiles_lon):
        along_x(d, mom_x_send, mom_x.at[d - 1], mxs, mxr).wait_send()

        @pl.when(has_points(col))
        def _():
            along_x(d, ctl_send.at[pl.ds(0, share), :], ctl_x.at[d - 1], cxs, cxr).wait_send()


def results_kernel(grad, surf, ctrl, grad_out, surf_out, ctrl_out, sems):
    half = grad.shape[1] // 2
    pairs = [(surf, surf_out), (ctrl, ctrl_out)]
    for s in range(2):
        for part in (slice(0, half), slice(half, grad.shape[1])):
            pairs.append((grad.at[s, part], grad_out.at[s, part]))
    moves = [pltpu.make_async_copy(src, dst, sems.at[i]) for i, (src, dst) in enumerate(pairs)]
    for move in moves:
        move.start()
    for move in moves:
        move.wait()


def per_device(
    tracer_adjoint, surface_adjoint, flow_east, flow_north, vertical_mix, land_mask,
    conduct_east, conduct_north, surface_diagonal, pressure_load, surface_forcing,
    control_map, control_weight,
):
    tiles_lon, tiles_lat = lax.axis_size("gx"), lax.axis_size("gy")
    _, levels, cy, cx = tracer_adjoint.shape
    pack = -(-2 * levels // 8) * 8
    controls = CTRL_DEV * tiles_lon * tiles_lat
    points = control_map.shape[0]
    vmem = pl.BlockSpec(memory_space=pltpu.VMEM)
    hbm = pl.BlockSpec(memory_space=pltpu.HBM)
    dma = pltpu.SemaphoreType.DMA
    buf = lambda *shape: pltpu.VMEM(shape, F32)
    scratch = [
        buf(2, levels, cy, cx), buf(cy, cx), buf(levels, cy, cx), buf(levels, cy, cx),
        buf(levels - 1, cy, cx), pltpu.VMEM((levels, cy, cx), jnp.int32),
        pltpu.SMEM((2, levels), F32), pltpu.SMEM((2, levels), F32),
        pltpu.VMEM((points // LANES, LANES), jnp.int32), buf(points // LANES, LANES), dma((13,)),
        buf(4, levels, cy, cx), buf(levels, cy, cx), buf(4, cy, cx),
        buf(4, cy, cx), buf(4, cy, cx), buf(4, 8, cx), buf(4, 8, cx), buf(4, 4, 8, cx),
        buf(5, cy, cx), buf(3, pack, cx), buf(2, pack, cx),
        buf(4, cy, cx), buf(5, cy, cx), buf(2, pack, cx), buf(3, pack, cx),
        buf(8, cx), buf(tiles_lat - 1, 8, cx), buf(8, cx), buf(tiles_lon - 1, 8, cx),
        buf(6, cy, cx), buf(4, pack, cx),
        pltpu.VMEM((2 * LANES, 3 * LANES), jnp.bfloat16),
        pltpu.VMEM((controls, 2 * LANES), jnp.bfloat16),
        buf(controls, LANES), buf(tiles_lon - 1, controls // tiles_lon, LANES),
        buf(tiles_lat, SLOT, LANES), buf(tiles_lat - 1, SLOT, LANES),
        dma((8,)), dma((8,)), dma((4,)), dma((4,)),
        dma((tiles_lat - 1,)), dma((tiles_lat - 1,)), dma((tiles_lon - 1,)), dma((tiles_lon - 1,)),
        dma((tiles_lon - 1,)), dma((tiles_lon - 1,)), dma((tiles_lat - 1,)), dma((tiles_lat - 1,)),
    ]
    grad, surf, ctrl = pl.pallas_call(
        functools.partial(step_kernel, tiles_lon, tiles_lat, levels),
        out_shape=(
            pltpu.VMEM(tracer_adjoint.shape, F32),
            pltpu.VMEM(surface_adjoint.shape, F32),
            pltpu.VMEM((CTRL_DEV, 2, levels), F32),
        ),
        in_specs=[hbm] * 13,
        out_specs=(vmem, vmem, vmem),
        scratch_shapes=scratch,
        compiler_params=pltpu.CompilerParams(
            collective_id=0, has_side_effects=True, vmem_limit_bytes=VMEM_LIMIT),
    )(
        tracer_adjoint, surface_adjoint, flow_east, flow_north, vertical_mix, land_mask,
        conduct_east, conduct_north, surface_diagonal, pressure_load, surface_forcing,
        control_map.reshape(-1, LANES), control_weight.reshape(-1, LANES),
    )
    grad, surf, ctrl = pl.pallas_call(
        results_kernel,
        out_shape=tuple(jax.ShapeDtypeStruct(a.shape, F32) for a in (grad, surf, ctrl)),
        in_specs=[pl.BlockSpec(memory_space=pl.ANY)] * 3,
        out_specs=(hbm, hbm, hbm),
        scratch_shapes=[dma((6,))],
        compiler_params=pltpu.CompilerParams(vmem_limit_bytes=1024 * 1024),
    )(grad, surf, ctrl)
    return grad, surf, ctrl.transpose(1, 2, 0)


def solution(mesh):
    in_specs = (
        P(None, None, "gy", "gx"), P("gy", "gx"),
        P(None, "gy", "gx"), P(None, "gy", "gx"), P(None, "gy", "gx"), P(None, "gy", "gx"),
        P("gy", "gx"), P("gy", "gx"), P("gy", "gx"), P(), P(), P(), P(),
    )
    out_specs = (P(None, None, "gy", "gx"), P("gy", "gx"), P(None, None, ("gx", "gy")))
    return jax.shard_map(
        per_device, mesh=mesh, in_specs=in_specs, out_specs=out_specs, check_vma=False
    )
```

```python
import functools
import jax
import jax.numpy as jnp
from jax import lax
from jax.experimental import pallas as pl
from jax.experimental.pallas import tpu as pltpu
from jax.sharding import PartitionSpec as P

ITERS = 3
CTRL_DEV = 10
SLOT = 16
VMEM_LIMIT = 63_200 * 1024
LANES = 128
MESH = pl.DeviceIdType.MESH
DIRS = ((1, 0), (-1, 0), (0, 1), (0, -1), (1, 1), (-1, 1), (1, -1), (-1, -1))
OPPOSITE = (1, 0, 3, 2, 7, 6, 5, 4)
F32 = jnp.float32
HIGHEST = lax.Precision.HIGHEST


def unrolled(count, body, carry):
    width = max(u for u in range(1, 8) if count % u == 0)

    def several(i, carry):
        for u in range(width):
            carry = body(i * width + u, carry)
        return carry

    return lax.fori_loop(0, count // width, several, carry)


def column_roll(value, shift):
    return pltpu.roll(value, shift, 1)


def surface_apply(e, ce, cn, dg):
    rows, cols = e.shape
    flux_e = ce * (e - pltpu.roll(e, cols - 1, 1))
    flux_n = cn * (e - pltpu.roll(e, rows - 1, 0))
    return dg * e + (flux_e - pltpu.roll(flux_e, 1, 1)) + (flux_n - pltpu.roll(flux_n, 1, 0))


def poly_add(p, q, factor):
    size = max(len(p), len(q))
    out = []
    for i in range(size):
        term = factor * q[i] if i < len(q) else None
        if i < len(p):
            term = p[i] if term is None else p[i] + term
        out.append(term)
    return out


def gradient_weights(mu):
    def inner(p, q, shift):
        total = None
        for i, pi in enumerate(p):
            for j, qj in enumerate(q):
                term = pi * qj * mu[i + j + shift]
                total = term if total is None else total + term
        return total

    one = jnp.ones_like(mu[0])
    zero = jnp.zeros_like(mu[0])
    floor = 2e-7 * mu[0]
    res, search, x = [one], [one], [zero]
    rr = mu[0]
    for it in range(ITERS):
        den = inner(search, search, 1)
        good = (den > 0) & (rr > floor)
        step = jnp.where(good, rr / jnp.where(good, den, one), zero)
        x = poly_add(x, search, step)
        if it + 1 < ITERS:
            res = poly_add(res, [zero] + search, -step)
            rr_new = jnp.maximum(inner(res, res, 0), zero)
            ratio = jnp.where(good, rr_new / jnp.where(good, rr, one), zero)
            search = poly_add(res, search, ratio)
            rr = rr_new
    return x


def step_kernel(
    tiles_lon, tiles_lat, levels,
    tracer_in, surface_in, flow_e_in, flow_n_in, mix_in, mask_in, cond_e_in, cond_n_in, diag_in,
    load_in, forcing_in, cmap_in, cwt_in,
    grad_out, surf_out, ctrl_out,
    tracer, surface, flow_e, flow_n, mix, mask, load, forcing, cmap, cwt, ins,
    red, ratio, quad, q_e, q_w, q_n, q_s, q_c,
    pk, send_n, send_s, recv_e, recv_w, recv_n, recv_s,
    mom_send, mom_y, mom_x_send, mom_x,
    pr, rr, parts, hot,
    ctl_send, ctl_x, ctl_y_send, ctl_y,
    hs, hr, ls, lr, mys, myr, mxs, mxr, cxs, cxr, cys, cyr,
):
    col = lax.axis_index("gx")
    row = lax.axis_index("gy")
    cy, cx = surface.shape
    moves = [
        pltpu.make_async_copy(src, dst, ins.at[i])
        for i, (src, dst) in enumerate((
            (forcing_in, forcing), (mask_in, mask), (tracer_in, tracer), (surface_in, surface),
            (cond_e_in, quad.at[1]), (cond_n_in, quad.at[2]), (diag_in, quad.at[3]),
            (load_in, load), (mix_in, mix), (flow_e_in, flow_e), (flow_n_in, flow_n),
            (cmap_in, cmap), (cwt_in, cwt)))
    ]
    for move in moves:
        move.start()

    has = []
    for dx, dy in DIRS:
        ok = None
        for d, pos, size in ((dx, col, tiles_lon), (dy, row, tiles_lat)):
            if d:
                here = (pos < size - 1) if d > 0 else (pos > 0)
                ok = here if ok is None else ok & here
        has.append(ok)

    barrier = pltpu.get_barrier_semaphore()
    for d in range(1, tiles_lon):
        pl.semaphore_signal(barrier, inc=1, device_id=(lax.rem(col + d, tiles_lon), row), device_id_type=MESH)
    for d in range(1, tiles_lat):
        pl.semaphore_signal(barrier, inc=1, device_id=(col, lax.rem(row + d, tiles_lat)), device_id_type=MESH)
    for i in range(4, 8):
        dx, dy = DIRS[i]

        @pl.when(has[i])
        def _():
            pl.semaphore_signal(barrier, inc=1, device_id=(col + dx, row + dy), device_id_type=MESH)

    q_slots = [q_e, q_w, q_n, q_s] + [q_c.at[i] for i in range(4)]
    for i, slot in enumerate(q_slots):

        @pl.when(jnp.logical_not(has[i]))
        def _():
            slot[...] = jnp.zeros(slot.shape, F32)

    l_slots = [recv_e, recv_w, recv_n, recv_s]
    for i, slot in enumerate(l_slots):

        @pl.when(jnp.logical_not(has[i]))
        def _():
            slot[...] = jnp.zeros(slot.shape, F32)

    for buf in (pk, send_n, send_s, pr, rr):
        buf[...] = jnp.zeros(buf.shape, F32)

    for move in moves[:4]:
        move.wait()

    lane = lax.broadcasted_iota(jnp.int32, (cy, cx), 1)

    def forcing_level(k, acc):
        wet = mask[k].astype(F32)
        return acc + wet * (forcing[0, k] * tracer[0, k] + forcing[1, k] * tracer[1, k])

    quad[0] = unrolled(levels, forcing_level, surface[...])
    for move in moves[4:7]:
        move.wait()

    n_signals = tiles_lon - 1 + tiles_lat - 1
    total = jnp.int32(n_signals)
    for i in range(4, 8):
        total = total + has[i].astype(jnp.int32)
    pl.semaphore_wait(barrier, total)

    q_src = [
        quad, quad, quad.at[:, cy - 8 : cy, :], quad.at[:, 0:8, :],
        quad.at[:, cy - 8 : cy, :], quad.at[:, cy - 8 : cy, :],
        quad.at[:, 0:8, :], quad.at[:, 0:8, :],
    ]

    def q_copy(i):
        dx, dy = DIRS[i]
        o = OPPOSITE[i]
        return pltpu.make_async_remote_copy(
            src_ref=q_src[i], dst_ref=q_slots[o], send_sem=hs.at[i], recv_sem=hr.at[o],
            device_id=(col + dx, row + dy), device_id_type=MESH)

    def q_arrival(i):
        dx, dy = DIRS[i]
        return pltpu.make_async_remote_copy(
            src_ref=q_slots[i], dst_ref=q_slots[i], send_sem=hs.at[i], recv_sem=hr.at[i],
            device_id=(col + dx, row + dy), device_id_type=MESH)

    for i in range(8):

        @pl.when(has[i])
        def _():
            q_copy(i).start()

    quarter = levels // 16 * 4
    bounds = (levels, 3 * quarter, 2 * quarter, quarter, 0)
    l_table = [
        (0, pk.at[4], recv_w.at[4]), (2, send_n.at[2], recv_s.at[2]),
        (0, pk.at[0:4], recv_w.at[0:4]), (1, pk.at[0:4], recv_e),
    ]
    for high, low in zip(bounds[:-1], bounds[1:]):
        rows = pl.ds(2 * low, (send_s.shape[1] if high == levels else 2 * high) - 2 * low)
        l_table.append((2, send_n.at[0:2, rows, :], recv_s.at[0:2, rows, :]))
        l_table.append((3, send_s.at[0:2, rows, :], recv_n.at[0:2, rows, :]))

    def l_copy(e):
        i, src, dst = l_table[e]
        dx, dy = DIRS[i]
        return pltpu.make_async_remote_copy(
            src_ref=src, dst_ref=dst, send_sem=ls.at[e], recv_sem=lr.at[e],
            device_id=(col + dx, row + dy), device_id_type=MESH)

    def l_start(e):
        @pl.when(has[l_table[e][0]])
        def _():
            l_copy(e).start()

    def l_arrive(e):
        o = OPPOSITE[l_table[e][0]]
        dst = l_table[e][2]
        dx, dy = DIRS[o]

        @pl.when(has[o])
        def _():
            pltpu.make_async_remote_copy(
                src_ref=dst, dst_ref=dst, send_sem=ls.at[e], recv_sem=lr.at[e],
                device_id=(col + dx, row + dy), device_id_type=MESH).wait_recv()

    west, south = col == 0, row == 0
    east_side = jnp.where(west, 0, 1)
    lon, lat = tiles_lon * cx, tiles_lat * cy
    controls = ctl_send.shape[0]
    lane_row = lax.broadcasted_iota(jnp.int32, (1, LANES), 1)
    last_chunk = cmap.shape[0] - 1

    def points(ref, begin):
        chunk = begin // LANES
        off = lax.rem(begin, LANES)
        near = ref[pl.ds(chunk, 1), :]
        far = ref[pl.ds(jnp.minimum(chunk + 1, last_chunk), 1), :]
        back = lax.rem(LANES - off, LANES)
        return jnp.where(
            lane_row < LANES - off, pltpu.roll(near, back, 1), pltpu.roll(far, back, 1))

    for move in moves[11:]:
        move.wait()
    begin_row = col * cx + jnp.where(south, 0, lon)
    begin_col = 2 * lon + row * cy + jnp.where(west, 0, lat)
    row_on = jnp.where(south | (row == tiles_lat - 1), 1.0, 0.0)
    col_on = jnp.where(west | (col == tiles_lon - 1), 1.0, 0.0)
    control_ids = lax.broadcasted_iota(jnp.int32, (controls, LANES), 0)
    for i, begin in enumerate((begin_row, begin_col)):
        hit = jnp.where(control_ids == points(cmap, begin), 1.0, 0.0)
        hot[:, i * LANES : (i + 1) * LANES] = hit.astype(jnp.bfloat16)
    row_wts = points(cwt, begin_row) * row_on
    diagonal = lax.broadcasted_iota(jnp.int32, (cy, LANES), 0) == lax.broadcasted_iota(
        jnp.int32, (cy, LANES), 1)
    col_wts = jnp.sum(
        jnp.where(diagonal, points(cwt, begin_col) * col_on, 0.0), axis=1, keepdims=True)

    def forward(k, kap, carry):
        kap_prev, ratio_prev, r0, r1, r2, r3 = carry
        wet = mask[k].astype(F32)
        inv = 1.0 / (1.0 + kap + kap_prev * (1.0 - ratio_prev))
        new_ratio = kap * inv
        r0 = (tracer[0, k] + kap_prev * r0) * inv
        r1 = (tracer[1, k] + kap_prev * r1) * inv
        r2 = (wet * load[0, k] + kap_prev * r2) * inv
        r3 = (wet * load[1, k] + kap_prev * r3) * inv
        ratio[k] = new_ratio
        red[0, k] = r0
        red[1, k] = r1
        red[2, k] = r2
        red[3, k] = r3
        pk[4] = jnp.where(pair == k, column_roll(flow_e[k], 2 * k + 1), pk[4])
        pr[4] = jnp.where(pair == k, column_roll(flow_e[k], 2 * k + 1 + 2 * east_side), pr[4])
        pr[5] = jnp.where(pair == k, column_roll(flow_n[k], 2 * k + 1 + east_side), pr[5])
        send_n[2, pl.ds(2 * k + 1, 1), :] = flow_n[k, cy - 1 : cy, :]
        face_e = jnp.where(south, flow_e[k, 0:1, :], flow_e[k, cy - 1 : cy, :])
        face_n = jnp.where(south, flow_n[k, 0:1, :], flow_n[k, cy - 2 : cy - 1, :])
        for s in range(2):
            rr[2, pl.ds(2 * k + 1 - s, 1), :] = face_e
            rr[3, pl.ds(2 * k + 1 - s, 1), :] = face_n
        return kap, new_ratio, r0, r1, r2, r3

    def forward_level(k, carry):
        return forward(k, mix[k] * mask[k + 1].astype(F32), carry)

    for move in moves[7:11]:
        move.wait()
    pair = lane // 2
    zero = jnp.zeros((cy, cx), F32)
    carry = unrolled(levels - 1, forward_level, (zero,) * 6)
    forward(levels - 1, zero, carry)
    l_start(0)
    l_start(1)

    for i in range(8):

        @pl.when(has[i])
        def _():
            q_arrival(i).wait_recv()

    lane8 = lax.broadcasted_iota(jnp.int32, (8, cx), 1) < cx // 2
    sub8 = lax.broadcasted_iota(jnp.int32, (8, cx), 0) < 4
    lane_half = lane < cx // 2

    def extend(f):
        side = jnp.where(lane_half, q_e[f], q_w[f])
        ends = jnp.where(sub8, q_n[f], q_s[f])
        corner = jnp.where(
            sub8, jnp.where(lane8, q_c[0, f], q_c[1, f]), jnp.where(lane8, q_c[2, f], q_c[3, f]))
        return jnp.concatenate(
            [jnp.concatenate([quad[f], ends], axis=0), jnp.concatenate([side, corner], axis=0)], axis=1)

    v0, ce, cn, dg = extend(0), extend(1), extend(2), extend(3)
    v1 = surface_apply(v0, ce, cn, dg)
    v2 = surface_apply(v1, ce, cn, dg)
    v3 = surface_apply(v2, ce, cn, dg)
    o0, o1, o2, o3 = (v[:cy, :cx] for v in (v0, v1, v2, v3))
    pairs = ((o0, o0), (o0, o1), (o1, o1), (o1, o2), (o2, o2), (o2, o3))
    mom_send[...] = jnp.concatenate(
        [jnp.sum(a * b, axis=0, keepdims=True) for a, b in pairs] + [jnp.zeros((2, cx), F32)], axis=0)

    def along_y(d, src, dst, ssem, rsem):
        return pltpu.make_async_remote_copy(
            src_ref=src, dst_ref=dst, send_sem=ssem.at[d - 1], recv_sem=rsem.at[d - 1],
            device_id=(col, lax.rem(row + d, tiles_lat)), device_id_type=MESH)

    def along_x(d, src, dst, ssem, rsem):
        return pltpu.make_async_remote_copy(
            src_ref=src, dst_ref=dst, send_sem=ssem.at[d - 1], recv_sem=rsem.at[d - 1],
            device_id=(lax.rem(col + d, tiles_lon), row), device_id_type=MESH)

    for d in range(1, tiles_lat):
        along_y(d, mom_send, mom_y.at[d - 1], mys, myr).start()

    def backward_level(first, step, carry):
        k = levels - 1 - first - step
        c = list(carry)
        wet = mask[k].astype(F32)
        rat = ratio[k]
        for f in range(4):
            c[f] = red[f, k] + rat * c[f]
            lam = wet * c[f]
            red[f, k] = lam
            kind, s = f // 2, f % 2
            idx = 2 * k + 1 - s
            pr[f] = jnp.where(pair == k, column_roll(lam, 2 * k + 3 * east_side), pr[f])
            pk[f] = jnp.where(pair == k, column_roll(lam, 2 * k + 1), pk[f])
            send_s[kind, pl.ds(idx, 1), :] = lam[0:1]
            send_n[kind, pl.ds(idx, 1), :] = lam[cy - 1 : cy]
            rr[kind, pl.ds(idx, 1), :] = jnp.where(south, lam[1:2], lam[cy - 2 : cy - 1])
        return tuple(c)

    columns = (zero,) * 4
    for part_no, (high, low) in enumerate(zip(bounds[:-1], bounds[1:])):
        columns = unrolled(
            high - low, functools.partial(backward_level, levels - high), columns)
        l_start(4 + 2 * part_no)
        l_start(5 + 2 * part_no)
        if part_no == 1:
            part = mom_send[...]
            for d in range(1, tiles_lat):
                along_y(d, mom_send, mom_y.at[d - 1], mys, myr).wait_recv()
            for d in range(1, tiles_lat):
                part = part + mom_y[d - 1]
            mom_x_send[...] = part
            for d in range(1, tiles_lon):
                along_x(d, mom_x_send, mom_x.at[d - 1], mxs, mxr).start()
    l_start(2)
    l_start(3)

    for d in range(1, tiles_lon):
        along_x(d, mom_x_send, mom_x.at[d - 1], mxs, mxr).wait_recv()
    for d in range(1, tiles_lon):
        part = part + mom_x[d - 1]
    sums = jnp.sum(part, axis=1, keepdims=True)
    w0, w1, w2 = gradient_weights([sums[i : i + 1] for i in range(6)])
    x = w0 * v0 + w1 * v1 + w2 * v2
    x_own = x[:cy, :cx]
    surf_out[...] = x_own

    for e in range(len(l_table)):
        l_arrive(e)

    even = lane == 2 * pair
    x_e, x_w = x[:cy, cx : cx + 1], x[:cy, 2 * cx - 1 : 2 * cx]
    for s in range(2):
        recv_e[s] = jnp.where(
            even,
            column_roll(recv_e[s] + x_e * recv_e[2 + s], cx - 1),
            column_roll(recv_w[s] + x_w * recv_w[2 + s], 1))
    recv_n[0] = recv_n[0] + x[cy : cy + 1, :cx] * recv_n[1]
    recv_s[0] = recv_s[0] + x[cy + 7 : cy + 8, :cx] * recv_s[1]

    sub = lax.broadcasted_iota(jnp.int32, (cy, cx), 0)
    first_lane, last_lane = lane == 0, lane == cx - 1
    first_row, last_row = sub == 0, sub == cy - 1

    filler = jnp.zeros((LANES - recv_n.shape[1], LANES), F32)

    def rim_lanes(rows):
        turned = jnp.concatenate([rows, filler], axis=0).T
        return jnp.where(west, turned[0:1], turned[cx - 1 : cx])

    north_row, south_row, south_face = (
        rim_lanes(recv_n[0]), rim_lanes(recv_s[0]), rim_lanes(recv_s[2]))
    x_rim = jnp.where(west, x[:cy, 0:1], x[:cy, cx - 1 : cx])
    x_in = jnp.where(west, x[:cy, 1:2], x[:cy, cx - 2 : cx - 1])
    half_sign = jnp.where(west, 0.5, -0.5)
    rim_cols = []
    for s in range(2):
        lam = pk[s] + x_rim * pk[2 + s]
        lam = jnp.where(west, lam, column_roll(lam, 1))
        inner = pr[s] + x_in * pr[2 + s]
        beyond_n = column_roll(north_row, 1) if s else north_row
        beyond_s = column_roll(south_row, 1) if s else south_row
        lam_n = jnp.where(last_row, beyond_n, pltpu.roll(lam, cy - 1, 0))
        flux_n = 0.5 * pr[5] * (lam_n - lam)
        flux_s = jnp.where(
            first_row, 0.5 * south_face * (lam - beyond_s), pltpu.roll(flux_n, 1, 0))
        rim_cols.append(lam + half_sign * pr[4] * (inner - lam) + flux_n + flux_s)
    by_col = jnp.where(even, column_roll(rim_cols[1], LANES - 1), rim_cols[0]) * col_wts
    by_col = jnp.concatenate([by_col, jnp.zeros((LANES - cy, LANES), F32)], axis=0)

    side_rows = [jnp.where(south, recv_e[s, 0:1, :], recv_e[s, cy - 1 : cy, :]) for s in range(2)]
    west_face = jnp.where(south, recv_w[4, 0:1, :], recv_w[4, cy - 1 : cy, :])
    even_row = even[0:1]
    turned = jnp.concatenate([
        jnp.where(even_row, side_rows[1], column_roll(side_rows[0], 1)),
        jnp.where(even_row, column_roll(side_rows[1], LANES - 1), side_rows[0]),
        jnp.where(even_row, west_face, column_roll(west_face, 1)),
        jnp.zeros((LANES - 3, LANES), F32)], axis=0).T[: rr.shape[1]]
    x_rim = jnp.where(south, x[0:1, :cx], x[cy - 1 : cy, :cx])
    x_in = jnp.where(south, x[1:2, :cx], x[cy - 2 : cy - 1, :cx])
    half_sign = jnp.where(south, 0.5, -0.5)
    lam = jnp.where(south, send_s[0], send_n[0]) + x_rim * jnp.where(south, send_s[1], send_n[1])
    inner = rr[0] + x_in * rr[1]
    lane_tall = lax.broadcasted_iota(jnp.int32, lam.shape, 1)
    lam_e = jnp.where(lane_tall == cx - 1, turned[:, 0:1], column_roll(lam, cx - 1))
    flux_e = 0.5 * rr[2] * (lam_e - lam)
    flux_w = jnp.where(
        lane_tall == 0, 0.5 * turned[:, 2:3] * (lam - turned[:, 1:2]), column_roll(flux_e, 1))
    by_row = (lam + half_sign * rr[3] * (inner - lam) + flux_e + flux_w) * row_wts
    by_row = jnp.concatenate([by_row, filler], axis=0).T

    for i, values in enumerate((by_row, by_col)):
        high = values.astype(jnp.bfloat16)
        rest = values - high.astype(F32)
        middle = rest.astype(jnp.bfloat16)
        low = (rest - middle.astype(F32)).astype(jnp.bfloat16)
        parts[i * LANES : (i + 1) * LANES] = jnp.concatenate([high, middle, low], axis=1)
    totals = lax.dot_general(
        hot[...], parts[...], (((1,), (0,)), ((), ())), preferred_element_type=F32)
    ctl_send[...] = (totals[:, 2 * LANES :] + totals[:, LANES : 2 * LANES]) + totals[:, :LANES]

    share = controls // tiles_lon

    def has_points(c):
        return south | (row == tiles_lat - 1) | (c == 0) | (c == tiles_lon - 1)

    for d in range(1, tiles_lon):
        begin = pl.multiple_of(lax.rem(col + d, tiles_lon) * share, 8)

        @pl.when(has_points(col))
        def _():
            along_x(d, ctl_send.at[pl.ds(begin, share), :], ctl_x.at[d - 1], cxs, cxr).start()

    def final_level(first, step, carry):
        k = first + step
        half_e = 0.5 * flow_e[k]
        half_n = 0.5 * flow_n[k]
        half_w_halo = 0.5 * column_roll(recv_w[4], lax.rem(cx - 2 * k, cx))
        half_s_halo = 0.5 * recv_s[2, pl.ds(2 * k + 1, 1), :]
        for s in range(2):
            idx = 2 * k + 1 - s
            lam = red[s, k] + x_own * red[2 + s, k]
            side = column_roll(recv_e[s], cx - 1 - 2 * k)
            lam_e = jnp.where(last_lane, side, column_roll(lam, cx - 1))
            lam_n = jnp.where(last_row, recv_n[0, pl.ds(idx, 1), :], pltpu.roll(lam, cy - 1, 0))
            flux_e = half_e * (lam_e - lam)
            flux_n = half_n * (lam_n - lam)
            halo_w = half_w_halo * (lam - side)
            halo_s = half_s_halo * (lam[0:1] - recv_s[0, pl.ds(idx, 1), :])
            flux_w = jnp.where(first_lane, halo_w, column_roll(flux_e, 1))
            flux_s = jnp.where(first_row, halo_s, pltpu.roll(flux_n, 1, 0))
            g = lam + flux_e + flux_w + flux_n + flux_s
            grad_out[s, k] = g
        return carry

    early = levels // 2
    unrolled(early, functools.partial(final_level, 0), 0)
    mine = ctl_send[pl.ds(pl.multiple_of(col * share, 8), share), :]
    for d in range(1, tiles_lon):
        sender = has_points(lax.rem(col + tiles_lon - d, tiles_lon))

        @pl.when(sender)
        def _():
            along_x(d, ctl_send.at[pl.ds(0, share), :], ctl_x.at[d - 1], cxs, cxr).wait_recv()

        @pl.when(jnp.logical_not(sender))
        def _():
            ctl_x[d - 1] = jnp.zeros((share, LANES), F32)

    for d in range(1, tiles_lon):
        mine = mine + ctl_x[d - 1]
    ctl_y_send[...] = jnp.zeros(ctl_y_send.shape, F32)
    for j in range(tiles_lat):
        ctl_y_send[j, 0:CTRL_DEV] = mine[j * CTRL_DEV : (j + 1) * CTRL_DEV]
    for d in range(1, tiles_lat):
        along_y(d, ctl_y_send.at[lax.rem(row + d, tiles_lat)], ctl_y.at[d - 1], cys, cyr).start()
    unrolled(levels - early, functools.partial(final_level, early), 0)
    result = ctl_y_send[row]
    for d in range(1, tiles_lat):
        along_y(d, ctl_y_send.at[0], ctl_y.at[d - 1], cys, cyr).wait_recv()
    for d in range(1, tiles_lat):
        result = result + ctl_y[d - 1]
    source = lax.broadcasted_iota(jnp.int32, (LANES, LANES), 0)
    target = lax.broadcasted_iota(jnp.int32, (LANES, LANES), 1)
    order = jnp.where(target < levels, 2 * target + 1, 2 * (target - levels))
    result = lax.dot_general(
        result, jnp.where(source == order, 1.0, 0.0), (((1,), (0,)), ((), ())),
        precision=HIGHEST, preferred_element_type=F32)
    for s in range(2):
        ctrl_out[:, s, :] = result[0:CTRL_DEV, s * levels : (s + 1) * levels]

    for i in range(8):

        @pl.when(has[i])
        def _():
            q_copy(i).wait_send()

    for e in range(len(l_table)):

        @pl.when(has[l_table[e][0]])
        def _():
            l_copy(e).wait_send()

    for d in range(1, tiles_lat):
        along_y(d, mom_send, mom_y.at[d - 1], mys, myr).wait_send()
        along_y(d, ctl_y_send.at[0], ctl_y.at[d - 1], cys, cyr).wait_send()
    for d in range(1, tiles_lon):
        along_x(d, mom_x_send, mom_x.at[d - 1], mxs, mxr).wait_send()

        @pl.when(has_points(col))
        def _():
            along_x(d, ctl_send.at[pl.ds(0, share), :], ctl_x.at[d - 1], cxs, cxr).wait_send()


def results_kernel(grad, surf, ctrl, grad_out, surf_out, ctrl_out, sems):
    half = grad.shape[1] // 2
    pairs = [(surf, surf_out), (ctrl, ctrl_out)]
    for s in range(2):
        for part in (slice(0, half), slice(half, grad.shape[1])):
            pairs.append((grad.at[s, part], grad_out.at[s, part]))
    moves = [pltpu.make_async_copy(src, dst, sems.at[i]) for i, (src, dst) in enumerate(pairs)]
    for move in moves:
        move.start()
    for move in moves:
        move.wait()


def per_device(
    tracer_adjoint, surface_adjoint, flow_east, flow_north, vertical_mix, land_mask,
    conduct_east, conduct_north, surface_diagonal, pressure_load, surface_forcing,
    control_map, control_weight,
):
    tiles_lon, tiles_lat = lax.axis_size("gx"), lax.axis_size("gy")
    _, levels, cy, cx = tracer_adjoint.shape
    pack = -(-2 * levels // 8) * 8
    controls = CTRL_DEV * tiles_lon * tiles_lat
    points = control_map.shape[0]
    vmem = pl.BlockSpec(memory_space=pltpu.VMEM)
    hbm = pl.BlockSpec(memory_space=pltpu.HBM)
    dma = pltpu.SemaphoreType.DMA
    buf = lambda *shape: pltpu.VMEM(shape, F32)
    scratch = [
        buf(2, levels, cy, cx), buf(cy, cx), buf(levels, cy, cx), buf(levels, cy, cx),
        buf(levels - 1, cy, cx), pltpu.VMEM((levels, cy, cx), jnp.int32),
        pltpu.SMEM((2, levels), F32), pltpu.SMEM((2, levels), F32),
        pltpu.VMEM((points // LANES, LANES), jnp.int32), buf(points // LANES, LANES), dma((13,)),
        buf(4, levels, cy, cx), buf(levels, cy, cx), buf(4, cy, cx),
        buf(4, cy, cx), buf(4, cy, cx), buf(4, 8, cx), buf(4, 8, cx), buf(4, 4, 8, cx),
        buf(5, cy, cx), buf(3, pack, cx), buf(2, pack, cx),
        buf(4, cy, cx), buf(5, cy, cx), buf(2, pack, cx), buf(3, pack, cx),
        buf(8, cx), buf(tiles_lat - 1, 8, cx), buf(8, cx), buf(tiles_lon - 1, 8, cx),
        buf(6, cy, cx), buf(4, pack, cx),
        pltpu.VMEM((2 * LANES, 3 * LANES), jnp.bfloat16),
        pltpu.VMEM((controls, 2 * LANES), jnp.bfloat16),
        buf(controls, LANES), buf(tiles_lon - 1, controls // tiles_lon, LANES),
        buf(tiles_lat, SLOT, LANES), buf(tiles_lat - 1, SLOT, LANES),
        dma((8,)), dma((8,)), dma((12,)), dma((12,)),
        dma((tiles_lat - 1,)), dma((tiles_lat - 1,)), dma((tiles_lon - 1,)), dma((tiles_lon - 1,)),
        dma((tiles_lon - 1,)), dma((tiles_lon - 1,)), dma((tiles_lat - 1,)), dma((tiles_lat - 1,)),
    ]
    grad, surf, ctrl = pl.pallas_call(
        functools.partial(step_kernel, tiles_lon, tiles_lat, levels),
        out_shape=(
            pltpu.VMEM(tracer_adjoint.shape, F32),
            pltpu.VMEM(surface_adjoint.shape, F32),
            pltpu.VMEM((CTRL_DEV, 2, levels), F32),
        ),
        in_specs=[hbm] * 13,
        out_specs=(vmem, vmem, vmem),
        scratch_shapes=scratch,
        compiler_params=pltpu.CompilerParams(
            collective_id=0, has_side_effects=True, vmem_limit_bytes=VMEM_LIMIT),
    )(
        tracer_adjoint, surface_adjoint, flow_east, flow_north, vertical_mix, land_mask,
        conduct_east, conduct_north, surface_diagonal, pressure_load, surface_forcing,
        control_map.reshape(-1, LANES), control_weight.reshape(-1, LANES),
    )
    grad, surf, ctrl = pl.pallas_call(
        results_kernel,
        out_shape=tuple(jax.ShapeDtypeStruct(a.shape, F32) for a in (grad, surf, ctrl)),
        in_specs=[pl.BlockSpec(memory_space=pl.ANY)] * 3,
        out_specs=(hbm, hbm, hbm),
        scratch_shapes=[dma((6,))],
        compiler_params=pltpu.CompilerParams(vmem_limit_bytes=1024 * 1024),
    )(grad, surf, ctrl)
    return grad, surf, ctrl.transpose(1, 2, 0)


def solution(mesh):
    in_specs = (
        P(None, None, "gy", "gx"), P("gy", "gx"),
        P(None, "gy", "gx"), P(None, "gy", "gx"), P(None, "gy", "gx"), P(None, "gy", "gx"),
        P("gy", "gx"), P("gy", "gx"), P("gy", "gx"), P(), P(), P(), P(),
    )
    out_specs = (P(None, None, "gy", "gx"), P("gy", "gx"), P(None, None, ("gx", "gy")))
    return jax.shard_map(
        per_device, mesh=mesh, in_specs=in_specs, out_specs=out_specs, check_vma=False
    )
```

```python
import functools
import jax
import jax.numpy as jnp
from jax import lax
from jax.experimental import pallas as pl
from jax.experimental.pallas import tpu as pltpu
from jax.sharding import PartitionSpec as P

ITERS = 3
CTRL_DEV = 10
SLOT = 16
VMEM_LIMIT = 63_200 * 1024
LANES = 128
MESH = pl.DeviceIdType.MESH
DIRS = ((1, 0), (-1, 0), (0, 1), (0, -1), (1, 1), (-1, 1), (1, -1), (-1, -1))
OPPOSITE = (1, 0, 3, 2, 7, 6, 5, 4)
F32 = jnp.float32
HIGHEST = lax.Precision.HIGHEST


def step_width(count):
    return max(u for u in range(1, 8) if count % u == 0)


def unrolled(count, body, carry):
    width = step_width(count)

    def several(i, carry):
        for u in range(width):
            carry = body(i * width + u, carry)
        return carry

    return lax.fori_loop(0, count // width, several, carry)


def column_roll(value, shift):
    return pltpu.roll(value, shift, 1)


def surface_apply(e, ce, cn, dg):
    rows, cols = e.shape
    flux_e = ce * (e - pltpu.roll(e, cols - 1, 1))
    flux_n = cn * (e - pltpu.roll(e, rows - 1, 0))
    return dg * e + (flux_e - pltpu.roll(flux_e, 1, 1)) + (flux_n - pltpu.roll(flux_n, 1, 0))


def poly_add(p, q, factor):
    size = max(len(p), len(q))
    out = []
    for i in range(size):
        term = factor * q[i] if i < len(q) else None
        if i < len(p):
            term = p[i] if term is None else p[i] + term
        out.append(term)
    return out


def gradient_weights(mu):
    def inner(p, q, shift):
        total = None
        for i, pi in enumerate(p):
            for j, qj in enumerate(q):
                term = pi * qj * mu[i + j + shift]
                total = term if total is None else total + term
        return total

    one = jnp.ones_like(mu[0])
    zero = jnp.zeros_like(mu[0])
    floor = 2e-7 * mu[0]
    res, search, x = [one], [one], [zero]
    rr = mu[0]
    for it in range(ITERS):
        den = inner(search, search, 1)
        good = (den > 0) & (rr > floor)
        step = jnp.where(good, rr / jnp.where(good, den, one), zero)
        x = poly_add(x, search, step)
        if it + 1 < ITERS:
            res = poly_add(res, [zero] + search, -step)
            rr_new = jnp.maximum(inner(res, res, 0), zero)
            ratio = jnp.where(good, rr_new / jnp.where(good, rr, one), zero)
            search = poly_add(res, search, ratio)
            rr = rr_new
    return x


def step_kernel(
    tiles_lon, tiles_lat, levels,
    tracer_in, surface_in, flow_e_in, flow_n_in, mix_in, mask_in, cond_e_in, cond_n_in, diag_in,
    load_in, forcing_in, cmap_in, cwt_in,
    grad_out, surf_out, ctrl_out,
    tracer, surface, flow_e, flow_n, mix, mask, load, forcing, cmap, cwt, ins,
    red, ratio, quad, q_e, q_w, q_n, q_s, q_c,
    pk, send_n, send_s, recv_e, recv_w, recv_n, recv_s,
    mom_send, mom_y, mom_x_send, mom_x,
    pr, rr, parts, hot,
    ctl_send, ctl_x, ctl_y_send, ctl_y,
    hs, hr, ls, lr, mys, myr, mxs, mxr, cxs, cxr, cys, cyr,
):
    col = lax.axis_index("gx")
    row = lax.axis_index("gy")
    cy, cx = surface.shape
    moves = [
        pltpu.make_async_copy(src, dst, ins.at[i])
        for i, (src, dst) in enumerate((
            (forcing_in, forcing), (mask_in, mask), (tracer_in, tracer), (surface_in, surface),
            (cond_e_in, quad.at[1]), (cond_n_in, quad.at[2]), (diag_in, quad.at[3]),
            (load_in, load), (mix_in, mix), (flow_e_in, flow_e), (flow_n_in, flow_n),
            (cmap_in, cmap), (cwt_in, cwt)))
    ]
    for move in moves:
        move.start()

    has = []
    for dx, dy in DIRS:
        ok = None
        for d, pos, size in ((dx, col, tiles_lon), (dy, row, tiles_lat)):
            if d:
                here = (pos < size - 1) if d > 0 else (pos > 0)
                ok = here if ok is None else ok & here
        has.append(ok)

    barrier = pltpu.get_barrier_semaphore()
    for d in range(1, tiles_lon):
        pl.semaphore_signal(barrier, inc=1, device_id=(lax.rem(col + d, tiles_lon), row), device_id_type=MESH)
    for d in range(1, tiles_lat):
        pl.semaphore_signal(barrier, inc=1, device_id=(col, lax.rem(row + d, tiles_lat)), device_id_type=MESH)
    for i in range(4, 8):
        dx, dy = DIRS[i]

        @pl.when(has[i])
        def _():
            pl.semaphore_signal(barrier, inc=1, device_id=(col + dx, row + dy), device_id_type=MESH)

    q_slots = [q_e, q_w, q_n, q_s] + [q_c.at[i] for i in range(4)]
    for i, slot in enumerate(q_slots):

        @pl.when(jnp.logical_not(has[i]))
        def _():
            slot[...] = jnp.zeros(slot.shape, F32)

    l_slots = [recv_e, recv_w, recv_n, recv_s]
    for i, slot in enumerate(l_slots):

        @pl.when(jnp.logical_not(has[i]))
        def _():
            slot[...] = jnp.zeros(slot.shape, F32)

    for buf in (pk, send_n, send_s, pr, rr):
        buf[...] = jnp.zeros(buf.shape, F32)

    for move in moves[:4]:
        move.wait()

    lane = lax.broadcasted_iota(jnp.int32, (cy, cx), 1)

    def forcing_level(k, acc):
        wet = mask[k].astype(F32)
        return acc + wet * (forcing[0, k] * tracer[0, k] + forcing[1, k] * tracer[1, k])

    quad[0] = unrolled(levels, forcing_level, surface[...])
    for move in moves[4:7]:
        move.wait()

    n_signals = tiles_lon - 1 + tiles_lat - 1
    total = jnp.int32(n_signals)
    for i in range(4, 8):
        total = total + has[i].astype(jnp.int32)
    pl.semaphore_wait(barrier, total)

    q_src = [
        quad, quad, quad.at[:, cy - 8 : cy, :], quad.at[:, 0:8, :],
        quad.at[:, cy - 8 : cy, :], quad.at[:, cy - 8 : cy, :],
        quad.at[:, 0:8, :], quad.at[:, 0:8, :],
    ]

    def q_copy(i):
        dx, dy = DIRS[i]
        o = OPPOSITE[i]
        return pltpu.make_async_remote_copy(
            src_ref=q_src[i], dst_ref=q_slots[o], send_sem=hs.at[i], recv_sem=hr.at[o],
            device_id=(col + dx, row + dy), device_id_type=MESH)

    def q_arrival(i):
        dx, dy = DIRS[i]
        return pltpu.make_async_remote_copy(
            src_ref=q_slots[i], dst_ref=q_slots[i], send_sem=hs.at[i], recv_sem=hr.at[i],
            device_id=(col + dx, row + dy), device_id_type=MESH)

    for i in range(8):

        @pl.when(has[i])
        def _():
            q_copy(i).start()

    quarter = levels // 16 * 4
    bounds = (levels, 3 * quarter, 2 * quarter, quarter, 0)
    l_table = [
        (0, pk.at[4], recv_w.at[4]), (2, send_n.at[2], recv_s.at[2]),
        (0, pk.at[0:4], recv_w.at[0:4]), (1, pk.at[0:4], recv_e),
    ]
    for high, low in zip(bounds[:-1], bounds[1:]):
        rows = pl.ds(2 * low, (send_s.shape[1] if high == levels else 2 * high) - 2 * low)
        l_table.append((2, send_n.at[0:2, rows, :], recv_s.at[0:2, rows, :]))
        l_table.append((3, send_s.at[0:2, rows, :], recv_n.at[0:2, rows, :]))

    def l_copy(e):
        i, src, dst = l_table[e]
        dx, dy = DIRS[i]
        return pltpu.make_async_remote_copy(
            src_ref=src, dst_ref=dst, send_sem=ls.at[e], recv_sem=lr.at[e],
            device_id=(col + dx, row + dy), device_id_type=MESH)

    def l_start(e):
        @pl.when(has[l_table[e][0]])
        def _():
            l_copy(e).start()

    def l_arrive(e):
        o = OPPOSITE[l_table[e][0]]
        dst = l_table[e][2]
        dx, dy = DIRS[o]

        @pl.when(has[o])
        def _():
            pltpu.make_async_remote_copy(
                src_ref=dst, dst_ref=dst, send_sem=ls.at[e], recv_sem=lr.at[e],
                device_id=(col + dx, row + dy), device_id_type=MESH).wait_recv()

    west, south = col == 0, row == 0
    east_side = jnp.where(west, 0, 1)
    lon, lat = tiles_lon * cx, tiles_lat * cy
    controls = ctl_send.shape[0]
    lane_row = lax.broadcasted_iota(jnp.int32, (1, LANES), 1)
    last_chunk = cmap.shape[0] - 1

    def points(ref, begin):
        chunk = begin // LANES
        off = lax.rem(begin, LANES)
        near = ref[pl.ds(chunk, 1), :]
        far = ref[pl.ds(jnp.minimum(chunk + 1, last_chunk), 1), :]
        back = lax.rem(LANES - off, LANES)
        return jnp.where(
            lane_row < LANES - off, pltpu.roll(near, back, 1), pltpu.roll(far, back, 1))

    for move in moves[11:]:
        move.wait()
    begin_row = col * cx + jnp.where(south, 0, lon)
    begin_col = 2 * lon + row * cy + jnp.where(west, 0, lat)
    row_on = jnp.where(south | (row == tiles_lat - 1), 1.0, 0.0)
    col_on = jnp.where(west | (col == tiles_lon - 1), 1.0, 0.0)
    control_ids = lax.broadcasted_iota(jnp.int32, (controls, LANES), 0)
    for i, begin in enumerate((begin_row, begin_col)):
        hit = jnp.where(control_ids == points(cmap, begin), 1.0, 0.0)
        hot[:, i * LANES : (i + 1) * LANES] = hit.astype(jnp.bfloat16)
    row_wts = points(cwt, begin_row) * row_on
    diagonal = lax.broadcasted_iota(jnp.int32, (cy, LANES), 0) == lax.broadcasted_iota(
        jnp.int32, (cy, LANES), 1)
    col_wts = jnp.sum(
        jnp.where(diagonal, points(cwt, begin_col) * col_on, 0.0), axis=1, keepdims=True)

    def forward(k, kap, carry):
        kap_prev, ratio_prev, r0, r1, r2, r3 = carry
        wet = mask[k].astype(F32)
        inv = 1.0 / (1.0 + kap + kap_prev * (1.0 - ratio_prev))
        new_ratio = kap * inv
        r0 = (tracer[0, k] + kap_prev * r0) * inv
        r1 = (tracer[1, k] + kap_prev * r1) * inv
        r2 = (wet * load[0, k] + kap_prev * r2) * inv
        r3 = (wet * load[1, k] + kap_prev * r3) * inv
        ratio[k] = new_ratio
        red[0, k] = r0
        red[1, k] = r1
        red[2, k] = r2
        red[3, k] = r3
        pk[4] = jnp.where(pair == k, column_roll(flow_e[k], 2 * k + 1), pk[4])
        pr[4] = jnp.where(pair == k, column_roll(flow_e[k], 2 * k + 1 + 2 * east_side), pr[4])
        pr[5] = jnp.where(pair == k, column_roll(flow_n[k], 2 * k + 1 + east_side), pr[5])
        send_n[2, pl.ds(2 * k + 1, 1), :] = flow_n[k, cy - 1 : cy, :]
        face_e = jnp.where(south, flow_e[k, 0:1, :], flow_e[k, cy - 1 : cy, :])
        face_n = jnp.where(south, flow_n[k, 0:1, :], flow_n[k, cy - 2 : cy - 1, :])
        for s in range(2):
            rr[2, pl.ds(2 * k + 1 - s, 1), :] = face_e
            rr[3, pl.ds(2 * k + 1 - s, 1), :] = face_n
        return kap, new_ratio, r0, r1, r2, r3

    def forward_level(k, carry):
        return forward(k, mix[k] * mask[k + 1].astype(F32), carry)

    for move in moves[7:11]:
        move.wait()
    pair = lane // 2
    zero = jnp.zeros((cy, cx), F32)
    carry = unrolled(levels - 1, forward_level, (zero,) * 6)
    forward(levels - 1, zero, carry)
    l_start(0)
    l_start(1)

    for i in range(8):

        @pl.when(has[i])
        def _():
            q_arrival(i).wait_recv()

    lane8 = lax.broadcasted_iota(jnp.int32, (8, cx), 1) < cx // 2
    sub8 = lax.broadcasted_iota(jnp.int32, (8, cx), 0) < 4
    lane_half = lane < cx // 2

    def extend(f):
        side = jnp.where(lane_half, q_e[f], q_w[f])
        ends = jnp.where(sub8, q_n[f], q_s[f])
        corner = jnp.where(
            sub8, jnp.where(lane8, q_c[0, f], q_c[1, f]), jnp.where(lane8, q_c[2, f], q_c[3, f]))
        return jnp.concatenate(
            [jnp.concatenate([quad[f], ends], axis=0), jnp.concatenate([side, corner], axis=0)], axis=1)

    v0, ce, cn, dg = extend(0), extend(1), extend(2), extend(3)
    v1 = surface_apply(v0, ce, cn, dg)
    v2 = surface_apply(v1, ce, cn, dg)
    v3 = surface_apply(v2, ce, cn, dg)
    o0, o1, o2, o3 = (v[:cy, :cx] for v in (v0, v1, v2, v3))
    pairs = ((o0, o0), (o0, o1), (o1, o1), (o1, o2), (o2, o2), (o2, o3))
    mom_send[...] = jnp.concatenate(
        [jnp.sum(a * b, axis=0, keepdims=True) for a, b in pairs] + [jnp.zeros((2, cx), F32)], axis=0)

    def along_y(d, src, dst, ssem, rsem):
        return pltpu.make_async_remote_copy(
            src_ref=src, dst_ref=dst, send_sem=ssem.at[d - 1], recv_sem=rsem.at[d - 1],
            device_id=(col, lax.rem(row + d, tiles_lat)), device_id_type=MESH)

    def along_x(d, src, dst, ssem, rsem):
        return pltpu.make_async_remote_copy(
            src_ref=src, dst_ref=dst, send_sem=ssem.at[d - 1], recv_sem=rsem.at[d - 1],
            device_id=(lax.rem(col + d, tiles_lon), row), device_id_type=MESH)

    for d in range(1, tiles_lat):
        along_y(d, mom_send, mom_y.at[d - 1], mys, myr).start()

    def backward_group(width, first, i, carry):
        c = list(carry)
        for f in range(4):
            kind, s = f // 2, f % 2
            outer, inner = pk[f], pr[f]
            for u in range(width):
                k = levels - 1 - first - (i * width + u)
                idx = 2 * k + 1 - s
                c[f] = red[f, k] + ratio[k] * c[f]
                lam = mask[k].astype(F32) * c[f]
                red[f, k] = lam
                inner = jnp.where(pair == k, column_roll(lam, 2 * k + 3 * east_side), inner)
                outer = jnp.where(pair == k, column_roll(lam, 2 * k + 1), outer)
                send_s[kind, pl.ds(idx, 1), :] = lam[0:1]
                send_n[kind, pl.ds(idx, 1), :] = lam[cy - 1 : cy]
                rr[kind, pl.ds(idx, 1), :] = jnp.where(south, lam[1:2], lam[cy - 2 : cy - 1])
            pk[f] = outer
            pr[f] = inner
        return tuple(c)

    columns = (zero,) * 4
    for part_no, (high, low) in enumerate(zip(bounds[:-1], bounds[1:])):
        width = step_width(high - low)
        columns = lax.fori_loop(
            0, (high - low) // width,
            functools.partial(backward_group, width, levels - high), columns)
        l_start(4 + 2 * part_no)
        l_start(5 + 2 * part_no)
        if part_no == 1:
            part = mom_send[...]
            for d in range(1, tiles_lat):
                along_y(d, mom_send, mom_y.at[d - 1], mys, myr).wait_recv()
            for d in range(1, tiles_lat):
                part = part + mom_y[d - 1]
            mom_x_send[...] = part
            for d in range(1, tiles_lon):
                along_x(d, mom_x_send, mom_x.at[d - 1], mxs, mxr).start()
    l_start(2)
    l_start(3)

    for d in range(1, tiles_lon):
        along_x(d, mom_x_send, mom_x.at[d - 1], mxs, mxr).wait_recv()
    for d in range(1, tiles_lon):
        part = part + mom_x[d - 1]
    sums = jnp.sum(part, axis=1, keepdims=True)
    w0, w1, w2 = gradient_weights([sums[i : i + 1] for i in range(6)])
    x = w0 * v0 + w1 * v1 + w2 * v2
    x_own = x[:cy, :cx]
    surf_out[...] = x_own

    for e in range(len(l_table)):
        l_arrive(e)

    even = lane == 2 * pair
    x_e, x_w = x[:cy, cx : cx + 1], x[:cy, 2 * cx - 1 : 2 * cx]
    for s in range(2):
        recv_e[s] = jnp.where(
            even,
            column_roll(recv_e[s] + x_e * recv_e[2 + s], cx - 1),
            column_roll(recv_w[s] + x_w * recv_w[2 + s], 1))
    recv_n[0] = recv_n[0] + x[cy : cy + 1, :cx] * recv_n[1]
    recv_s[0] = recv_s[0] + x[cy + 7 : cy + 8, :cx] * recv_s[1]

    sub = lax.broadcasted_iota(jnp.int32, (cy, cx), 0)
    first_lane, last_lane = lane == 0, lane == cx - 1
    first_row, last_row = sub == 0, sub == cy - 1

    filler = jnp.zeros((LANES - recv_n.shape[1], LANES), F32)

    def rim_lanes(rows):
        turned = jnp.concatenate([rows, filler], axis=0).T
        return jnp.where(west, turned[0:1], turned[cx - 1 : cx])

    north_row, south_row, south_face = (
        rim_lanes(recv_n[0]), rim_lanes(recv_s[0]), rim_lanes(recv_s[2]))
    x_rim = jnp.where(west, x[:cy, 0:1], x[:cy, cx - 1 : cx])
    x_in = jnp.where(west, x[:cy, 1:2], x[:cy, cx - 2 : cx - 1])
    half_sign = jnp.where(west, 0.5, -0.5)
    rim_cols = []
    for s in range(2):
        lam = pk[s] + x_rim * pk[2 + s]
        lam = jnp.where(west, lam, column_roll(lam, 1))
        inner = pr[s] + x_in * pr[2 + s]
        beyond_n = column_roll(north_row, 1) if s else north_row
        beyond_s = column_roll(south_row, 1) if s else south_row
        lam_n = jnp.where(last_row, beyond_n, pltpu.roll(lam, cy - 1, 0))
        flux_n = 0.5 * pr[5] * (lam_n - lam)
        flux_s = jnp.where(
            first_row, 0.5 * south_face * (lam - beyond_s), pltpu.roll(flux_n, 1, 0))
        rim_cols.append(lam + half_sign * pr[4] * (inner - lam) + flux_n + flux_s)
    by_col = jnp.where(even, column_roll(rim_cols[1], LANES - 1), rim_cols[0]) * col_wts
    by_col = jnp.concatenate([by_col, jnp.zeros((LANES - cy, LANES), F32)], axis=0)

    side_rows = [jnp.where(south, recv_e[s, 0:1, :], recv_e[s, cy - 1 : cy, :]) for s in range(2)]
    west_face = jnp.where(south, recv_w[4, 0:1, :], recv_w[4, cy - 1 : cy, :])
    even_row = even[0:1]
    turned = jnp.concatenate([
        jnp.where(even_row, side_rows[1], column_roll(side_rows[0], 1)),
        jnp.where(even_row, column_roll(side_rows[1], LANES - 1), side_rows[0]),
        jnp.where(even_row, west_face, column_roll(west_face, 1)),
        jnp.zeros((LANES - 3, LANES), F32)], axis=0).T[: rr.shape[1]]
    x_rim = jnp.where(south, x[0:1, :cx], x[cy - 1 : cy, :cx])
    x_in = jnp.where(south, x[1:2, :cx], x[cy - 2 : cy - 1, :cx])
    half_sign = jnp.where(south, 0.5, -0.5)
    lam = jnp.where(south, send_s[0], send_n[0]) + x_rim * jnp.where(south, send_s[1], send_n[1])
    inner = rr[0] + x_in * rr[1]
    lane_tall = lax.broadcasted_iota(jnp.int32, lam.shape, 1)
    lam_e = jnp.where(lane_tall == cx - 1, turned[:, 0:1], column_roll(lam, cx - 1))
    flux_e = 0.5 * rr[2] * (lam_e - lam)
    flux_w = jnp.where(
        lane_tall == 0, 0.5 * turned[:, 2:3] * (lam - turned[:, 1:2]), column_roll(flux_e, 1))
    by_row = (lam + half_sign * rr[3] * (inner - lam) + flux_e + flux_w) * row_wts
    by_row = jnp.concatenate([by_row, filler], axis=0).T

    for i, values in enumerate((by_row, by_col)):
        high = values.astype(jnp.bfloat16)
        rest = values - high.astype(F32)
        middle = rest.astype(jnp.bfloat16)
        low = (rest - middle.astype(F32)).astype(jnp.bfloat16)
        parts[i * LANES : (i + 1) * LANES] = jnp.concatenate([high, middle, low], axis=1)
    totals = lax.dot_general(
        hot[...], parts[...], (((1,), (0,)), ((), ())), preferred_element_type=F32)
    ctl_send[...] = (totals[:, 2 * LANES :] + totals[:, LANES : 2 * LANES]) + totals[:, :LANES]

    share = controls // tiles_lon

    def has_points(c):
        return south | (row == tiles_lat - 1) | (c == 0) | (c == tiles_lon - 1)

    for d in range(1, tiles_lon):
        begin = pl.multiple_of(lax.rem(col + d, tiles_lon) * share, 8)

        @pl.when(has_points(col))
        def _():
            along_x(d, ctl_send.at[pl.ds(begin, share), :], ctl_x.at[d - 1], cxs, cxr).start()

    def final_level(first, step, carry):
        k = first + step
        half_e = 0.5 * flow_e[k]
        half_n = 0.5 * flow_n[k]
        half_w_halo = 0.5 * column_roll(recv_w[4], lax.rem(cx - 2 * k, cx))
        half_s_halo = 0.5 * recv_s[2, pl.ds(2 * k + 1, 1), :]
        for s in range(2):
            idx = 2 * k + 1 - s
            lam = red[s, k] + x_own * red[2 + s, k]
            side = column_roll(recv_e[s], cx - 1 - 2 * k)
            lam_e = jnp.where(last_lane, side, column_roll(lam, cx - 1))
            lam_n = jnp.where(last_row, recv_n[0, pl.ds(idx, 1), :], pltpu.roll(lam, cy - 1, 0))
            flux_e = half_e * (lam_e - lam)
            flux_n = half_n * (lam_n - lam)
            halo_w = half_w_halo * (lam - side)
            halo_s = half_s_halo * (lam[0:1] - recv_s[0, pl.ds(idx, 1), :])
            flux_w = jnp.where(first_lane, halo_w, column_roll(flux_e, 1))
            flux_s = jnp.where(first_row, halo_s, pltpu.roll(flux_n, 1, 0))
            g = lam + flux_e + flux_w + flux_n + flux_s
            grad_out[s, k] = g
        return carry

    early = levels // 2
    unrolled(early, functools.partial(final_level, 0), 0)
    mine = ctl_send[pl.ds(pl.multiple_of(col * share, 8), share), :]
    for d in range(1, tiles_lon):
        sender = has_points(lax.rem(col + tiles_lon - d, tiles_lon))

        @pl.when(sender)
        def _():
            along_x(d, ctl_send.at[pl.ds(0, share), :], ctl_x.at[d - 1], cxs, cxr).wait_recv()

        @pl.when(jnp.logical_not(sender))
        def _():
            ctl_x[d - 1] = jnp.zeros((share, LANES), F32)

    for d in range(1, tiles_lon):
        mine = mine + ctl_x[d - 1]
    ctl_y_send[...] = jnp.zeros(ctl_y_send.shape, F32)
    for j in range(tiles_lat):
        ctl_y_send[j, 0:CTRL_DEV] = mine[j * CTRL_DEV : (j + 1) * CTRL_DEV]
    for d in range(1, tiles_lat):
        along_y(d, ctl_y_send.at[lax.rem(row + d, tiles_lat)], ctl_y.at[d - 1], cys, cyr).start()
    unrolled(levels - early, functools.partial(final_level, early), 0)
    result = ctl_y_send[row]
    for d in range(1, tiles_lat):
        along_y(d, ctl_y_send.at[0], ctl_y.at[d - 1], cys, cyr).wait_recv()
    for d in range(1, tiles_lat):
        result = result + ctl_y[d - 1]
    source = lax.broadcasted_iota(jnp.int32, (LANES, LANES), 0)
    target = lax.broadcasted_iota(jnp.int32, (LANES, LANES), 1)
    order = jnp.where(target < levels, 2 * target + 1, 2 * (target - levels))
    result = lax.dot_general(
        result, jnp.where(source == order, 1.0, 0.0), (((1,), (0,)), ((), ())),
        precision=HIGHEST, preferred_element_type=F32)
    for s in range(2):
        ctrl_out[:, s, :] = result[0:CTRL_DEV, s * levels : (s + 1) * levels]

    for i in range(8):

        @pl.when(has[i])
        def _():
            q_copy(i).wait_send()

    for e in range(len(l_table)):

        @pl.when(has[l_table[e][0]])
        def _():
            l_copy(e).wait_send()

    for d in range(1, tiles_lat):
        along_y(d, mom_send, mom_y.at[d - 1], mys, myr).wait_send()
        along_y(d, ctl_y_send.at[0], ctl_y.at[d - 1], cys, cyr).wait_send()
    for d in range(1, tiles_lon):
        along_x(d, mom_x_send, mom_x.at[d - 1], mxs, mxr).wait_send()

        @pl.when(has_points(col))
        def _():
            along_x(d, ctl_send.at[pl.ds(0, share), :], ctl_x.at[d - 1], cxs, cxr).wait_send()


def results_kernel(grad, surf, ctrl, grad_out, surf_out, ctrl_out, sems):
    half = grad.shape[1] // 2
    pairs = [(surf, surf_out), (ctrl, ctrl_out)]
    for s in range(2):
        for part in (slice(0, half), slice(half, grad.shape[1])):
            pairs.append((grad.at[s, part], grad_out.at[s, part]))
    moves = [pltpu.make_async_copy(src, dst, sems.at[i]) for i, (src, dst) in enumerate(pairs)]
    for move in moves:
        move.start()
    for move in moves:
        move.wait()


def per_device(
    tracer_adjoint, surface_adjoint, flow_east, flow_north, vertical_mix, land_mask,
    conduct_east, conduct_north, surface_diagonal, pressure_load, surface_forcing,
    control_map, control_weight,
):
    tiles_lon, tiles_lat = lax.axis_size("gx"), lax.axis_size("gy")
    _, levels, cy, cx = tracer_adjoint.shape
    pack = -(-2 * levels // 8) * 8
    controls = CTRL_DEV * tiles_lon * tiles_lat
    points = control_map.shape[0]
    vmem = pl.BlockSpec(memory_space=pltpu.VMEM)
    hbm = pl.BlockSpec(memory_space=pltpu.HBM)
    dma = pltpu.SemaphoreType.DMA
    buf = lambda *shape: pltpu.VMEM(shape, F32)
    scratch = [
        buf(2, levels, cy, cx), buf(cy, cx), buf(levels, cy, cx), buf(levels, cy, cx),
        buf(levels - 1, cy, cx), pltpu.VMEM((levels, cy, cx), jnp.int32),
        pltpu.SMEM((2, levels), F32), pltpu.SMEM((2, levels), F32),
        pltpu.VMEM((points // LANES, LANES), jnp.int32), buf(points // LANES, LANES), dma((13,)),
        buf(4, levels, cy, cx), buf(levels, cy, cx), buf(4, cy, cx),
        buf(4, cy, cx), buf(4, cy, cx), buf(4, 8, cx), buf(4, 8, cx), buf(4, 4, 8, cx),
        buf(5, cy, cx), buf(3, pack, cx), buf(2, pack, cx),
        buf(4, cy, cx), buf(5, cy, cx), buf(2, pack, cx), buf(3, pack, cx),
        buf(8, cx), buf(tiles_lat - 1, 8, cx), buf(8, cx), buf(tiles_lon - 1, 8, cx),
        buf(6, cy, cx), buf(4, pack, cx),
        pltpu.VMEM((2 * LANES, 3 * LANES), jnp.bfloat16),
        pltpu.VMEM((controls, 2 * LANES), jnp.bfloat16),
        buf(controls, LANES), buf(tiles_lon - 1, controls // tiles_lon, LANES),
        buf(tiles_lat, SLOT, LANES), buf(tiles_lat - 1, SLOT, LANES),
        dma((8,)), dma((8,)), dma((12,)), dma((12,)),
        dma((tiles_lat - 1,)), dma((tiles_lat - 1,)), dma((tiles_lon - 1,)), dma((tiles_lon - 1,)),
        dma((tiles_lon - 1,)), dma((tiles_lon - 1,)), dma((tiles_lat - 1,)), dma((tiles_lat - 1,)),
    ]
    grad, surf, ctrl = pl.pallas_call(
        functools.partial(step_kernel, tiles_lon, tiles_lat, levels),
        out_shape=(
            pltpu.VMEM(tracer_adjoint.shape, F32),
            pltpu.VMEM(surface_adjoint.shape, F32),
            pltpu.VMEM((CTRL_DEV, 2, levels), F32),
        ),
        in_specs=[hbm] * 13,
        out_specs=(vmem, vmem, vmem),
        scratch_shapes=scratch,
        compiler_params=pltpu.CompilerParams(
            collective_id=0, has_side_effects=True, vmem_limit_bytes=VMEM_LIMIT),
    )(
        tracer_adjoint, surface_adjoint, flow_east, flow_north, vertical_mix, land_mask,
        conduct_east, conduct_north, surface_diagonal, pressure_load, surface_forcing,
        control_map.reshape(-1, LANES), control_weight.reshape(-1, LANES),
    )
    grad, surf, ctrl = pl.pallas_call(
        results_kernel,
        out_shape=tuple(jax.ShapeDtypeStruct(a.shape, F32) for a in (grad, surf, ctrl)),
        in_specs=[pl.BlockSpec(memory_space=pl.ANY)] * 3,
        out_specs=(hbm, hbm, hbm),
        scratch_shapes=[dma((6,))],
        compiler_params=pltpu.CompilerParams(vmem_limit_bytes=1024 * 1024),
    )(grad, surf, ctrl)
    return grad, surf, ctrl.transpose(1, 2, 0)


def solution(mesh):
    in_specs = (
        P(None, None, "gy", "gx"), P("gy", "gx"),
        P(None, "gy", "gx"), P(None, "gy", "gx"), P(None, "gy", "gx"), P(None, "gy", "gx"),
        P("gy", "gx"), P("gy", "gx"), P("gy", "gx"), P(), P(), P(), P(),
    )
    out_specs = (P(None, None, "gy", "gx"), P("gy", "gx"), P(None, None, ("gx", "gy")))
    return jax.shard_map(
        per_device, mesh=mesh, in_specs=in_specs, out_specs=out_specs, check_vma=False
    )
```
